32 devices in a mesh: space: 16 (over z, x, core), mode: 2 (over y).
Axes of the slice: x: 2, y: 2, z: 4, core: 2. Of those that a mesh axis runs over, the one named last changes fastest.
Arguments:
- state: float32 [858, 4096], P(None, ('space', 'mode')), may hold values from -6 to 6
- tensor: bfloat16 [16, 286, 858], P('mode'), may hold values from -0.01171875 to 0.01171875
- table: int32 [286, 3], replicated, may hold values from 0 to 10, as said below
- thermal: float32 [3], replicated, may hold values from 0.5 to 2
- output_mode_row: int32 [16], replicated, may hold values from 0 to 857, as said below
Outputs:
- updated: float32 [858, 4096], P(None, ('space', 'mode'))
- collision: float32 [16, 4096], P('mode', 'space')
The draws below stay inside these ranges and needn't reach their ends.
Inputs may be any that keep to these rules, and one draw needn't show every extreme that they name: `table`: each row holds the three indices of one multi-index of total degree at most 10; every such multi-index is in exactly one row. `output_mode_row`: all entries are different.
All inputs are finite; a program needn't handle non-finite values.
Results may differ from the reference program's by a relative error of at most 0.004.
Values may be sent and summed in bfloat16 or wider, within the bound.
No kernel may reach another device: no remote copies, remote signals or barrier semaphores. Data moves between devices by JAX's collectives and lax.ppermute only.
A program may use at most 64 MiB of HBM per device.

```python
import math
import jax
import jax.numpy as jnp
import numpy as np
from jax import lax

DEGREE = 10
CLASSES = 3
MODES = 286
OUT = 16
CELLS = 4096


def draw_table(key, part):
    listing = []
    for along_x in range(DEGREE + 1):
        for along_y in range(DEGREE + 1 - along_x):
            for along_z in range(DEGREE + 1 - along_x - along_y):
                listing.append((along_x, along_y, along_z))
    canonical = jnp.asarray(np.array(listing, dtype=np.int32))
    ordering = jax.random.permutation(jax.random.fold_in(key, 7), canonical.shape[0])
    return canonical[ordering].astype(jnp.int32)


def draw_output_mode_row(key, part):
    ordering = jax.random.permutation(jax.random.fold_in(key, 11), CLASSES * MODES)
    return ordering[:OUT].astype(jnp.int32)


def block_scale(own_key, dims, pieces, low, high):
    def one(position, shards_of):
        steps = jax.random.uniform(jax.random.fold_in(jax.random.fold_in(own_key, 6), position), (shards_of,), jnp.float32, low / len(pieces), high / len(pieces))
        return jnp.repeat(jnp.exp(steps), dims[position] // shards_of).reshape((-1,) + (1,) * (len(dims) - position - 1))

    gain = one(*pieces[0])
    for cut in pieces[1:]:
        gain = gain * one(*cut)
    return gain


def noise(key, extent, deviation, most, split=(), kind=jnp.bfloat16):
    drawn = deviation * jax.random.normal(key, extent, jnp.float32)
    if split:
        drawn = drawn * block_scale(key, extent, split, -0.22, 0.18)
    return jnp.clip(drawn, -most, most).astype(kind)


def setup_inputs(seed: int = 0) -> dict:
    splits = jax.random.split(jax.random.key(seed), 6)
    return {
        "state": noise(splits[0], (CLASSES * MODES, CELLS), 1.0, 6.0, ((1, 32),), jnp.float32),
        "tensor": noise(splits[1], (OUT, MODES, CLASSES * MODES), (MODES * CLASSES * MODES) ** -0.5, 0.01171875, ((0, 2),)),
        "table": draw_table(jax.random.fold_in(splits[5], 71), 0),
        "thermal": jnp.clip(jnp.exp(jax.random.uniform(splits[3], (CLASSES,), jnp.float32, math.log(0.5), math.log(2.0))), 0.5, 2.0),
        "output_mode_row": draw_output_mode_row(jax.random.fold_in(splits[5], 71), 0),
    }


wave_bound = 5.2
courant = 0.09
collision_update = 0.1

def advection_matrix(table):
    codes = table[:, 0] * 144 + table[:, 1] * 12 + table[:, 2]
    along = table[:, 0].astype(jnp.float32)
    lower = (codes[None, :] == codes[:, None] - 144).astype(jnp.float32)
    higher = (codes[None, :] == codes[:, None] + 144).astype(jnp.float32)
    return jnp.sqrt(along)[:, None] * lower + jnp.sqrt(along + 1.0)[:, None] * higher

def upwind_transport(extended, state, matrix, thermal):
    blocks = extended.reshape(CLASSES, MODES, -1)
    state_after_collision = jnp.einsum('ab,cbx->cax', matrix, blocks, precision=lax.Precision.HIGHEST)
    speed = thermal[:, None, None]
    flux = 0.5 * speed * (state_after_collision[:, :, :-1] + state_after_collision[:, :, 1:]) - 0.5 * wave_bound * speed * (blocks[:, :, 1:] - blocks[:, :, :-1])
    change = (flux[:, :, 1:] - flux[:, :, :-1]).reshape(CLASSES * MODES, -1)
    return state - courant * change

def reference(state, tensor, table, thermal, output_mode_row):
    coarse = state.astype(jnp.bfloat16)

    def one_output(pair):
        weights, target = pair
        product = jnp.dot(weights, coarse, preferred_element_type=jnp.float32)
        start = (target // MODES * MODES).astype(jnp.int32)
        first = lax.dynamic_slice_in_dim(coarse, start, MODES, 0).astype(jnp.float32)
        return lax.optimization_barrier(jnp.sum(first * product, axis=0))
    collision = lax.map(one_output, (tensor, output_mode_row))
    matrix = advection_matrix(table)
    extended = jnp.concatenate([state[:, -1:], state, state[:, :1]], axis=1)
    advected_state = upwind_transport(extended, state, matrix, thermal)
    updated = advected_state.at[output_mode_row].add(collision_update * collision)
    return (updated, collision)
```

```python
import jax
import jax.numpy as jnp
from jax import lax
from jax.experimental import pallas as pl
from jax.experimental.pallas import tpu as pltpu
from jax.sharding import PartitionSpec as P

CLASSES = 3

wave_bound = 5.2
courant = 0.09
collision_update = 0.1

BF16 = jnp.bfloat16
F32 = jnp.float32
VMEM = pl.BlockSpec(memory_space=pltpu.VMEM)
HBM = pl.BlockSpec(memory_space=pltpu.HBM)
PARAMS = pltpu.CompilerParams(vmem_limit_bytes=16 * 2**20)


def remain(x):
    return pltpu.with_memory_space_constraint(x, pltpu.HBM)


def dot(a, b):
    return jnp.dot(a, b, preferred_element_type=F32)


def dot_general(a, b, da, db):
    return lax.dot_general(a, b, (((da,), (db,)), ((), ())), preferred_element_type=F32)


def halves(x):
    high = x.astype(BF16)
    return high, (x - high.astype(F32)).astype(BF16)


def iota(shape, axis):
    return lax.broadcasted_iota(jnp.int32, shape, axis)


def coarsen_kernel(state_hbm, coarse_ref, state_ref, sems):
    rows = state_ref.shape[0]
    cut = rows // 2 // 16 * 16
    copies = []
    for j, (start, size) in enumerate(((0, cut), (cut, rows - cut))):
        part = pl.ds(start, size)
        copies.append((part, pltpu.make_async_copy(state_hbm.at[part], state_ref.at[part], sems.at[j])))
        copies[-1][1].start()
    for part, copy in copies:
        copy.wait()
        coarse_ref[part] = state_ref[part].astype(BF16)


def coarsen(state):
    return pl.pallas_call(
        coarsen_kernel,
        in_specs=[HBM],
        out_shape=(pltpu.VMEM(state.shape, BF16), pltpu.VMEM(state.shape, F32)),
        out_specs=(VMEM,) * 2,
        scratch_shapes=[pltpu.SemaphoreType.DMA((2,))],
        compiler_params=PARAMS,
        name="coarsen",
    )(remain(state))


def steps_of(modes, terms):
    for count in range(min(32, modes), 0, -1):
        if modes % count == 0 and count * terms % 16 == 0:
            return modes // count
    return 1


def contract(tensor_ref, coarse_ref, wide_ref, class_ref, steps, ready=None):
    terms, columns = class_ref.shape
    modes = tensor_ref.shape[0] // terms
    wide_ref[...] = coarse_ref[...].astype(F32)
    count = modes // steps
    sums = [jnp.zeros((terms, columns), F32) for _ in range(CLASSES)]
    for j in range(steps):
        if ready is not None:
            ready(j)
        product = dot(tensor_ref[pl.ds(j * count * terms, count * terms)], coarse_ref[...])
        product = product.reshape(count, terms, columns)
        for c in range(CLASSES):
            first = wide_ref[pl.ds(c * modes + j * count, count)]
            sums[c] = sums[c] + jnp.sum(first[:, None, :] * product, axis=0)
    total = jnp.zeros((terms, columns), F32)
    for c in range(CLASSES):
        total = total + jnp.where(class_ref[...] == c, sums[c], 0.0)
    return total


def advection_halves(table_ref, high_ref, low_ref):
    modes = table_ref.shape[1]
    index = [table_ref[j : j + 1, :].astype(F32) for j in range(3)]
    row = iota((8, modes), 0)
    weighted = jnp.where(row == 0, 144.0 * index[0], jnp.where(row == 1, 12.0 * index[1], index[2]))
    weighted = jnp.where(row < 3, weighted, 0.0).astype(BF16)
    along = jnp.where(row == 0, index[0], 0.0).astype(BF16)
    ones = jnp.ones((8, modes), BF16)
    code_down = dot_general(weighted, ones, 0, 0)
    along_down = dot_general(along, ones, 0, 0)
    code_across = 144.0 * index[0] + 12.0 * index[1] + index[2]
    matrix = jnp.where(code_across == code_down - 144.0, jnp.sqrt(along_down), 0.0)
    matrix = matrix + jnp.where(code_across == code_down + 144.0, jnp.sqrt(along_down + 1.0), 0.0)
    high_ref[...], low_ref[...] = halves(matrix)


def own_work(hbm, coarse_ref, outs, scratch):
    tensor_hbm, table_hbm, thermal_hbm, target_hbm = hbm
    tensor_ref, own_ref, high_ref, low_ref, class_ref, here_ref, there_ref, speed_ref = outs
    wide_ref, table_ref, thermal_ref, target_ref, sems = scratch
    terms, columns = class_ref.shape
    rows, modes = coarse_ref.shape[0], high_ref.shape[0]
    outputs = target_ref.shape[0]
    pairs = (table_hbm, table_ref), (target_hbm, target_ref), (thermal_hbm, thermal_ref)
    small = [pltpu.make_async_copy(source, target, sems.at[j]) for j, (source, target) in enumerate(pairs)]
    for copy in small:
        copy.start()
    steps = sems.shape[0] - len(small)
    size = modes // steps * terms
    parts = []
    for j in range(steps):
        part = pl.ds(j * size, size)
        parts.append(pltpu.make_async_copy(tensor_hbm.at[part], tensor_ref.at[part], sems.at[len(small) + j]))
        parts[-1].start()
    for copy in small:
        copy.wait()
    first = lax.axis_index("mode") * terms
    for place_ref, start in ((here_ref, first), (there_ref, first + terms)):
        lane = iota(place_ref.shape, 1)
        target = jnp.zeros(place_ref.shape, jnp.int32)
        for j in range(place_ref.shape[1]):
            target = jnp.where(lane == j, target_ref[lax.rem(start + j, outputs)], target)
        place_ref[...] = (iota(place_ref.shape, 0) == target).astype(BF16)
    line = iota((terms, columns), 0)
    kind = jnp.zeros((terms, columns), jnp.int32)
    for j in range(terms):
        target = target_ref[first + j]
        own_class = sum((target >= c * modes).astype(jnp.int32) for c in range(1, CLASSES))
        kind = jnp.where(line == j, own_class, kind)
    class_ref[...] = kind
    line = iota(speed_ref.shape, 0)
    speed = jnp.zeros(speed_ref.shape, F32)
    for c in range(CLASSES):
        speed = jnp.where(line == c, thermal_ref[c], speed)
    speed_ref[...] = speed
    advection_halves(table_ref, high_ref, low_ref)
    own_ref[...] = contract(tensor_ref, coarse_ref, wide_ref, class_ref, steps, lambda j: parts[j].wait())


def at_seam():
    return jnp.logical_and(lax.axis_index("space") == 0, lax.axis_index("mode") == 0)


def early_kernel(coarse_ref, *refs):
    hbm, edge_ref, outs, scratch = refs[:4], refs[4], refs[5:13], refs[13:]
    columns = coarse_ref.shape[1]
    wanted = jnp.where(lax.axis_index("mode") == 0, 0, columns - 1)
    pick = (iota((edge_ref.shape[0], columns), 1) == wanted).astype(BF16)
    edge_ref[...] = dot_general(pick, coarse_ref[...], 1, 1).astype(BF16)

    @pl.when(at_seam())
    def _():
        own_work(hbm, coarse_ref, outs, scratch)


def late_kernel(coarse_ref, *refs):
    hbm, outs, scratch = refs[:4], refs[12:20], refs[20:]

    @pl.when(jnp.logical_not(at_seam()))
    def _():
        own_work(hbm, coarse_ref, outs, scratch)


def own_shapes(tensor, coarse, modes, outputs):
    rows, columns = coarse.shape
    terms = tensor.shape[0] // modes
    return (
        pltpu.VMEM(tensor.shape, BF16),
        pltpu.VMEM((terms, columns), F32),
        pltpu.VMEM((modes, modes), BF16),
        pltpu.VMEM((modes, modes), BF16),
        pltpu.VMEM((terms, columns), jnp.int32),
        pltpu.VMEM((rows, terms), BF16),
        pltpu.VMEM((rows, outputs - terms), BF16),
        pltpu.VMEM((8, columns), F32),
    )


def own_scratch(coarse, tensor, table, thermal, target):
    modes = table.shape[1]
    steps = steps_of(modes, tensor.shape[0] // modes)
    return [
        pltpu.VMEM(coarse.shape, F32),
        pltpu.VMEM(table.shape, jnp.int32),
        pltpu.SMEM(thermal.shape, F32),
        pltpu.SMEM(target.shape, jnp.int32),
        pltpu.SemaphoreType.DMA((3 + steps,)),
    ]


def early(coarse, tensor, table, thermal, target):
    shapes = own_shapes(tensor, coarse, table.shape[1], target.shape[0])
    return pl.pallas_call(
        early_kernel,
        in_specs=[VMEM] + [HBM] * 4,
        out_shape=(pltpu.VMEM((8, coarse.shape[0]), BF16),) + shapes,
        out_specs=(VMEM,) * (1 + len(shapes)),
        scratch_shapes=own_scratch(coarse, tensor, table, thermal, target),
        compiler_params=PARAMS,
        name="early_work",
    )(coarse, tensor, table, thermal, target)


def late(coarse, tensor, table, thermal, target, held):
    shapes = own_shapes(tensor, coarse, table.shape[1], target.shape[0])
    return pl.pallas_call(
        late_kernel,
        in_specs=[VMEM] + [HBM] * 4 + [VMEM] * len(held),
        out_shape=shapes,
        out_specs=(VMEM,) * len(shapes),
        scratch_shapes=own_scratch(coarse, tensor, table, thermal, target),
        input_output_aliases={5 + j: j for j in range(len(held))},
        compiler_params=PARAMS,
        name="late_work",
    )(coarse, tensor, table, thermal, target, *held)


def others_kernel(tensor_ref, coarse_ref, class_ref, collision_ref, sent_ref, wide_ref):
    terms = class_ref.shape[0]
    steps = steps_of(tensor_ref.shape[0] // terms, terms)
    total = contract(tensor_ref, coarse_ref, wide_ref, class_ref, steps)
    collision_ref[...] = total
    sent_ref[...] = total.astype(BF16)


def others_collision(tensor, coarse, class_of):
    return pl.pallas_call(
        others_kernel,
        in_specs=[VMEM] * 3,
        out_shape=(pltpu.VMEM(class_of.shape, F32), pltpu.VMEM(class_of.shape, BF16)),
        out_specs=(VMEM,) * 2,
        scratch_shapes=[pltpu.VMEM(coarse.shape, F32)],
        compiler_params=PARAMS,
        name="others_collision",
    )(tensor, coarse, class_of)


def transport_kernel(
    state_ref, high_ref, low_ref, speed_ref, ring_ref, left_ref, right_ref, own_ref, here_ref, *refs
):
    others, out_ref, collision_hbm, diff_ref, collision_ref, sem = refs[:-5], *refs[-5:]
    rows, columns = state_ref.shape
    modes = high_ref.shape[0]
    me, group = lax.axis_index("mode"), lax.axis_size("mode")
    for r, terms_ref in enumerate((own_ref, *others)):
        start = pl.multiple_of(lax.rem(me + group - r, group) * columns, columns)
        collision_ref[:, pl.ds(start, columns)] = terms_ref[...]
    copy = pltpu.make_async_copy(collision_ref, collision_hbm, sem)
    copy.start()
    state = state_ref[...]
    lane = iota((rows, columns), 1)
    ones = (iota((ring_ref.shape[0], columns), 0) == 0).astype(BF16)
    ring = dot_general(ring_ref[...], ones, 0, 0)
    left = jnp.where(me == 0, ring, pltpu.roll(left_ref[...].astype(F32), 1, 1))
    right = jnp.where(me == group - 1, ring, pltpu.roll(right_ref[...].astype(F32), columns - 1, 1))
    before = jnp.where(lane == 0, left, pltpu.roll(state, 1, 1))
    after = jnp.where(lane == columns - 1, right, pltpu.roll(state, columns - 1, 1))
    diff_ref[...] = after - before
    spread = before + after - 2.0 * state
    own_high, own_low = halves(own_ref[...])
    here = here_ref[...]
    out_ref[...] = state + collision_update * (dot(here, own_high) + dot(here, own_low))
    for c in range(CLASSES):
        part = pl.ds(c * modes, modes)
        speed = speed_ref[c : c + 1, :]
        d_high, d_low = halves(diff_ref[part])
        moved = dot(high_ref[...], d_high) + dot(high_ref[...], d_low) + dot(low_ref[...], d_high)
        diffused = (0.5 * wave_bound * courant) * spread[c * modes : (c + 1) * modes]
        out_ref[part] = out_ref[part] + speed * (diffused - (0.5 * courant) * moved)
    copy.wait()


def transport(state, high, low, speed, ring, left, right, own, here, others):
    terms, columns = own.shape
    collision = (terms, (1 + len(others)) * columns)
    return pl.pallas_call(
        transport_kernel,
        in_specs=[VMEM] * (9 + len(others)),
        out_shape=(pltpu.VMEM(state.shape, F32), jax.ShapeDtypeStruct(collision, F32)),
        out_specs=(VMEM, HBM),
        scratch_shapes=[pltpu.VMEM(state.shape, F32), pltpu.VMEM(collision, F32), pltpu.SemaphoreType.DMA],
        compiler_params=PARAMS,
        name="transport",
    )(state, high, low, speed, ring, left, right, own, here, *others)


def place_kernel(base_ref, there_ref, terms_ref, out_ref):
    out_ref[...] = base_ref[...] + collision_update * dot(there_ref[...], terms_ref[...])


def place_terms(base, there, terms):
    return pl.pallas_call(
        place_kernel,
        in_specs=[VMEM] * 3,
        out_shape=jax.ShapeDtypeStruct(base.shape, F32),
        out_specs=VMEM,
        compiler_params=PARAMS,
        name="place_terms",
    )(base, there, terms)


def shards(state, tensor, table, thermal, output_mode_row):
    rows, columns = state.shape
    terms, modes, _ = tensor.shape
    slabs, group = lax.axis_size("space"), lax.axis_size("mode")

    def shift(x, by):
        return lax.ppermute(x, "mode", [(i, (i + by) % group) for i in range(group)])

    coarse, wide = coarsen(state)
    cells = {r: shift(coarse, r) for r in range(1, group)}

    flat = jnp.transpose(tensor, (1, 0, 2)).reshape(modes * terms, rows)
    given = tuple(remain(x) for x in (flat, table.T, thermal, output_mode_row))
    edge, *held = early(coarse, *given)
    size = slabs * group
    pairs = [(s * group + group - 1, (s + 1) * group % size) for s in range(slabs)]
    ring = lax.ppermute(edge, ("space", "mode"), pairs + [(j, i) for i, j in pairs])
    held_tensor, own, high, low, class_of, here, there, speed = late(coarse, *given, held)

    returned, others = [], []
    for r in range(1, group):
        terms_of, sent = others_collision(held_tensor, cells[r], class_of)
        others.append(terms_of)
        returned.append(shift(sent, group - r))

    base, collision = transport(
        wide, high, low, speed, ring, cells[1], cells[group - 1], own, here, others
    )
    arrived = returned[0] if group == 2 else jnp.concatenate(returned)
    return place_terms(base, there, arrived), collision


def solution(mesh):
    in_specs = (P(None, ("space", "mode")), P("mode", None, None), P(), P(), P())
    out_specs = (P(None, ("space", "mode")), P("mode", "space"))
    return jax.shard_map(shards, mesh=mesh, in_specs=in_specs, out_specs=out_specs, check_vma=False)
```

```python
import jax
import jax.numpy as jnp
from jax import lax
from jax.experimental import pallas as pl
from jax.experimental.pallas import tpu as pltpu
from jax.sharding import PartitionSpec as P

CLASSES = 3

wave_bound = 5.2
courant = 0.09
collision_update = 0.1

BF16 = jnp.bfloat16
F32 = jnp.float32
VMEM = pl.BlockSpec(memory_space=pltpu.VMEM)
HBM = pl.BlockSpec(memory_space=pltpu.HBM)
PARAMS = pltpu.CompilerParams(vmem_limit_bytes=16 * 2**20)


def remain(x):
    return pltpu.with_memory_space_constraint(x, pltpu.HBM)


def dot(a, b):
    return jnp.dot(a, b, preferred_element_type=F32)


def dot_general(a, b, da, db):
    return lax.dot_general(a, b, (((da,), (db,)), ((), ())), preferred_element_type=F32)


def halves(x):
    high = x.astype(BF16)
    return high, (x - high.astype(F32)).astype(BF16)


def iota(shape, axis):
    return lax.broadcasted_iota(jnp.int32, shape, axis)


def coarsen_kernel(state_hbm, coarse_ref, state_ref, sems):
    rows = state_ref.shape[0]
    cut = rows // 2 // 16 * 16
    copies = []
    for j, (start, size) in enumerate(((0, cut), (cut, rows - cut))):
        part = pl.ds(start, size)
        copies.append((part, pltpu.make_async_copy(state_hbm.at[part], state_ref.at[part], sems.at[j])))
        copies[-1][1].start()
    for part, copy in copies:
        copy.wait()
        coarse_ref[part] = state_ref[part].astype(BF16)


def coarsen(state):
    return pl.pallas_call(
        coarsen_kernel,
        in_specs=[HBM],
        out_shape=(pltpu.VMEM(state.shape, BF16), pltpu.VMEM(state.shape, F32)),
        out_specs=(VMEM,) * 2,
        scratch_shapes=[pltpu.SemaphoreType.DMA((2,))],
        compiler_params=PARAMS,
        name="coarsen",
    )(remain(state))


def steps_of(modes, terms):
    for count in range(min(32, modes), 0, -1):
        if modes % count == 0 and count * terms % 16 == 0:
            return modes // count
    return 1


def contract(tensor_ref, cells_ref, wide_ref, class_ref, steps):
    terms, columns = class_ref.shape[0], cells_ref.shape[1]
    modes = tensor_ref.shape[0] // terms
    wide_ref[...] = cells_ref[...].astype(F32)
    count = modes // steps
    sums = [jnp.zeros((terms, columns), F32) for _ in range(CLASSES)]
    for j in range(steps):
        product = dot(tensor_ref[pl.ds(j * count * terms, count * terms)], cells_ref[...])
        product = product.reshape(count, terms, columns)
        for c in range(CLASSES):
            first = wide_ref[pl.ds(c * modes + j * count, count)]
            sums[c] = sums[c] + jnp.sum(first[:, None, :] * product, axis=0)
    total = jnp.zeros((terms, columns), F32)
    for c in range(CLASSES):
        total = total + jnp.where(class_ref[:, 0:1] == c, sums[c], 0.0)
    return total


def advection_halves(table_ref, high_ref, low_ref):
    modes = table_ref.shape[1]
    index = [table_ref[j : j + 1, :].astype(F32) for j in range(3)]
    row = iota((8, modes), 0)
    weighted = jnp.where(row == 0, 144.0 * index[0], jnp.where(row == 1, 12.0 * index[1], index[2]))
    weighted = jnp.where(row < 3, weighted, 0.0).astype(BF16)
    along = jnp.where(row == 0, index[0], 0.0).astype(BF16)
    ones = jnp.ones((8, modes), BF16)
    code_down = dot_general(weighted, ones, 0, 0)
    along_down = dot_general(along, ones, 0, 0)
    code_across = 144.0 * index[0] + 12.0 * index[1] + index[2]
    matrix = jnp.where(code_across == code_down - 144.0, jnp.sqrt(along_down), 0.0)
    matrix = matrix + jnp.where(code_across == code_down + 144.0, jnp.sqrt(along_down + 1.0), 0.0)
    high_ref[...], low_ref[...] = halves(matrix)


def fetch(hbm, outs, scratch):
    tensor_hbm, table_hbm, thermal_hbm, target_hbm = hbm
    tensor_ref, high_ref, low_ref, class_ref, here_ref, there_ref, speed_ref = outs
    table_ref, thermal_ref, target_ref, sems = scratch
    terms = class_ref.shape[0]
    modes = high_ref.shape[0]
    outputs = target_ref.shape[0]
    pairs = (table_hbm, table_ref), (target_hbm, target_ref), (thermal_hbm, thermal_ref)
    small = [pltpu.make_async_copy(source, target, sems.at[j]) for j, (source, target) in enumerate(pairs)]
    for copy in small:
        copy.start()
    whole = pltpu.make_async_copy(tensor_hbm, tensor_ref, sems.at[len(small)])
    whole.start()
    for copy in small:
        copy.wait()
    first = lax.axis_index("mode") * terms
    for place_ref, start in ((here_ref, first), (there_ref, first + terms)):
        lane = iota(place_ref.shape, 1)
        target = jnp.zeros(place_ref.shape, jnp.int32)
        for j in range(place_ref.shape[1]):
            target = jnp.where(lane == j, target_ref[lax.rem(start + j, outputs)], target)
        place_ref[...] = (iota(place_ref.shape, 0) == target).astype(BF16)
    line = iota(class_ref.shape, 0)
    kind = jnp.zeros(class_ref.shape, jnp.int32)
    for j in range(terms):
        target = target_ref[first + j]
        own_class = sum((target >= c * modes).astype(jnp.int32) for c in range(1, CLASSES))
        kind = jnp.where(line == j, own_class, kind)
    class_ref[...] = kind
    line = iota(speed_ref.shape, 0)
    speed = jnp.zeros(speed_ref.shape, F32)
    for c in range(CLASSES):
        speed = jnp.where(line == c, thermal_ref[c], speed)
    speed_ref[...] = speed
    advection_halves(table_ref, high_ref, low_ref)
    whole.wait()


def at_seam():
    return jnp.logical_and(lax.axis_index("space") == 0, lax.axis_index("mode") == 0)


def early_kernel(coarse_ref, *refs):
    hbm, edge_ref, outs, scratch = refs[:4], refs[4], refs[5:12], refs[12:]
    rows, columns = coarse_ref.shape
    wanted = jnp.where(lax.axis_index("mode") == 0, 0, columns - 1)
    pick = (iota((8, columns), 1) == wanted).astype(BF16)
    edge = dot_general(pick, coarse_ref[...], 1, 1)
    lines = []
    for start in range(0, rows, columns):
        line = edge[0:1, start : min(start + columns, rows)]
        if line.shape[1] < columns:
            line = jnp.concatenate([line, jnp.zeros((1, columns - line.shape[1]), F32)], axis=1)
        lines.append(line)
    lines += [jnp.zeros((1, columns), F32)] * (edge_ref.shape[0] - len(lines))
    edge_ref[...] = jnp.concatenate(lines, axis=0).astype(BF16)

    @pl.when(at_seam())
    def _():
        fetch(hbm, outs, scratch)


def late_kernel(state_ref, *refs):
    hbm, outs, moved_ref, scratch, diff_ref = refs[:4], refs[11:18], refs[18], refs[19:-1], refs[-1]

    @pl.when(jnp.logical_not(at_seam()))
    def _():
        fetch(hbm, outs, scratch)

    inner_transport(state_ref, outs[1], outs[2], outs[6], moved_ref, diff_ref)


def inner_transport(state_ref, high_ref, low_ref, speed_ref, out_ref, diff_ref):
    rows, columns = state_ref.shape
    modes = high_ref.shape[0]
    state = state_ref[...]
    lane = iota((rows, columns), 1)
    before = jnp.where(lane == 0, 0.0, pltpu.roll(state, 1, 1))
    after = jnp.where(lane == columns - 1, 0.0, pltpu.roll(state, columns - 1, 1))
    diff_ref[...] = after - before
    out_ref[...] = before + after - 2.0 * state
    for c in range(CLASSES):
        part = pl.ds(c * modes, modes)
        speed = speed_ref[c : c + 1, :]
        d_high, d_low = halves(diff_ref[part])
        moved = dot(high_ref[...], d_high) + dot(high_ref[...], d_low) + dot(low_ref[...], d_high)
        diffused = (0.5 * wave_bound * courant) * out_ref[part]
        out_ref[part] = state_ref[part] + speed * (diffused - (0.5 * courant) * moved)


def held_shapes(tensor, state, modes, outputs):
    rows, columns = state.shape
    terms = tensor.shape[0] // modes
    return (
        pltpu.VMEM(tensor.shape, BF16),
        pltpu.VMEM((modes, modes), BF16),
        pltpu.VMEM((modes, modes), BF16),
        pltpu.VMEM((terms, columns), jnp.int32),
        pltpu.VMEM((rows, terms), BF16),
        pltpu.VMEM((rows, outputs - terms), BF16),
        pltpu.VMEM((8, columns), F32),
    )


def fetch_scratch(table, thermal, target):
    return [
        pltpu.VMEM(table.shape, jnp.int32),
        pltpu.SMEM(thermal.shape, F32),
        pltpu.SMEM(target.shape, jnp.int32),
        pltpu.SemaphoreType.DMA((4,)),
    ]


def early(coarse, tensor, table, thermal, target):
    rows, columns = coarse.shape
    shapes = held_shapes(tensor, coarse, table.shape[1], target.shape[0])
    lines = -(-rows // columns // 8) * 8
    return pl.pallas_call(
        early_kernel,
        in_specs=[VMEM] + [HBM] * 4,
        out_shape=(pltpu.VMEM((lines, columns), BF16),) + shapes,
        out_specs=(VMEM,) * (1 + len(shapes)),
        scratch_shapes=fetch_scratch(table, thermal, target),
        compiler_params=PARAMS,
        name="early_fetch",
    )(coarse, tensor, table, thermal, target)


def late(state, tensor, table, thermal, target, held):
    shapes = held_shapes(tensor, state, table.shape[1], target.shape[0])
    return pl.pallas_call(
        late_kernel,
        in_specs=[VMEM] + [HBM] * 4 + [VMEM] * len(held),
        out_shape=shapes + (pltpu.VMEM(state.shape, F32),),
        out_specs=(VMEM,) * (1 + len(shapes)),
        scratch_shapes=fetch_scratch(table, thermal, target) + [pltpu.VMEM(state.shape, F32)],
        input_output_aliases={5 + j: j for j in range(len(held))},
        compiler_params=PARAMS,
        name="late_fetch",
    )(state, tensor, table, thermal, target, *held)


def collide_kernel(tensor_ref, class_ref, *refs):
    sets = (len(refs) - 2) // 3 + 1
    given, totals, sent, (cells_ref, wide_ref) = refs[:sets], refs[sets : 2 * sets], refs[2 * sets : -2], refs[-2:]
    terms, columns = class_ref.shape
    for j, ref in enumerate(given):
        cells_ref[:, j * columns : (j + 1) * columns] = ref[...]
    total = contract(tensor_ref, cells_ref, wide_ref, class_ref, steps_of(tensor_ref.shape[0] // terms, terms))
    for j, ref in enumerate(totals):
        ref[...] = total[:, j * columns : (j + 1) * columns]
    for j, ref in enumerate(sent, 1):
        ref[...] = total[:, j * columns : (j + 1) * columns].astype(BF16)


def collide(tensor, class_of, cells):
    sets = len(cells)
    rows, columns = cells[0].shape
    shapes = [pltpu.VMEM(class_of.shape, F32)] * sets + [pltpu.VMEM(class_of.shape, BF16)] * (sets - 1)
    found = pl.pallas_call(
        collide_kernel,
        in_specs=[VMEM] * (2 + sets),
        out_shape=tuple(shapes),
        out_specs=(VMEM,) * len(shapes),
        scratch_shapes=[pltpu.VMEM((rows, sets * columns), t) for t in (BF16, F32)],
        compiler_params=PARAMS,
        name="collide",
    )(tensor, class_of, *cells)
    return found[:sets], found[sets:]


def ends_kernel(inner_ref, high_ref, low_ref, speed_ref, ring_ref, left_ref, right_ref, here_ref, *refs):
    totals, out_ref, collision_hbm, beyond_ref, collision_ref, sem = refs[:-5], *refs[-5:]
    rows, columns = inner_ref.shape
    modes = high_ref.shape[0]
    me, group = lax.axis_index("mode"), lax.axis_size("mode")
    for r, terms_ref in enumerate(totals):
        start = pl.multiple_of(lax.rem(me + group - r, group) * columns, columns)
        collision_ref[:, pl.ds(start, columns)] = terms_ref[...]
    copy = pltpu.make_async_copy(collision_ref, collision_hbm, sem)
    copy.start()
    lane = iota((rows, columns), 1)
    ring = []
    for j, start in enumerate(range(0, rows, columns)):
        one = (iota((ring_ref.shape[0], columns), 0) == j).astype(BF16)
        ring.append(dot_general(ring_ref[...], one, 0, 0)[0 : min(columns, rows - start)])
    ring = jnp.concatenate(ring, axis=0)
    left = jnp.where(me == 0, ring, pltpu.roll(left_ref[...].astype(F32), 1, 1))
    right = jnp.where(me == group - 1, ring, pltpu.roll(right_ref[...].astype(F32), columns - 1, 1))
    beyond_ref[...] = jnp.where(lane == 0, left, jnp.where(lane == columns - 1, right, 0.0))
    own_high, own_low = halves(totals[0][...])
    here = here_ref[...]
    out_ref[...] = inner_ref[...] + collision_update * (dot(here, own_high) + dot(here, own_low))
    sign = jnp.where(iota((1, columns), 1) == 0, -1.0, 1.0)
    for c in range(CLASSES):
        part = pl.ds(c * modes, modes)
        speed = speed_ref[c : c + 1, :]
        value = beyond_ref[part]
        coarse = value.astype(BF16)
        moved = sign * (dot(high_ref[...], coarse) + dot(low_ref[...], coarse))
        out_ref[part] = out_ref[part] + speed * (
            (0.5 * wave_bound * courant) * value - (0.5 * courant) * moved
        )
    copy.wait()


def ends(inner, high, low, speed, ring, left, right, here, totals):
    terms, columns = totals[0].shape
    collision = (terms, len(totals) * columns)
    return pl.pallas_call(
        ends_kernel,
        in_specs=[VMEM] * (8 + len(totals)),
        out_shape=(pltpu.VMEM(inner.shape, F32), jax.ShapeDtypeStruct(collision, F32)),
        out_specs=(VMEM, HBM),
        scratch_shapes=[pltpu.VMEM(inner.shape, F32), pltpu.VMEM(collision, F32), pltpu.SemaphoreType.DMA],
        compiler_params=PARAMS,
        name="ends",
    )(inner, high, low, speed, ring, left, right, here, *totals)


def place_kernel(base_ref, there_ref, terms_ref, out_ref):
    out_ref[...] = base_ref[...] + collision_update * dot(there_ref[...], terms_ref[...])


def place_terms(base, there, terms):
    return pl.pallas_call(
        place_kernel,
        in_specs=[VMEM] * 3,
        out_shape=jax.ShapeDtypeStruct(base.shape, F32),
        out_specs=VMEM,
        compiler_params=PARAMS,
        name="place_terms",
    )(base, there, terms)


def shards(state, tensor, table, thermal, output_mode_row):
    rows, columns = state.shape
    terms, modes, _ = tensor.shape
    slabs, group = lax.axis_size("space"), lax.axis_size("mode")

    def shift(x, by):
        return lax.ppermute(x, "mode", [(i, (i + by) % group) for i in range(group)])

    coarse, wide = coarsen(state)
    cells = {r: shift(coarse, r) for r in range(1, group)}

    flat = jnp.transpose(tensor, (1, 0, 2)).reshape(modes * terms, rows)
    given = tuple(remain(x) for x in (flat, table.T, thermal, output_mode_row))
    edge, *held = early(coarse, *given)
    size = slabs * group
    pairs = [(s * group + group - 1, (s + 1) * group % size) for s in range(slabs)]
    ring = lax.ppermute(edge, ("space", "mode"), pairs + [(j, i) for i, j in pairs])
    held_tensor, high, low, class_of, here, there, speed, inner = late(wide, *given, held)

    totals, sent = collide(held_tensor, class_of, [coarse] + [cells[r] for r in range(1, group)])
    returned = [shift(x, group - r) for r, x in enumerate(sent, 1)]
    base, collision = ends(
        inner, high, low, speed, ring, cells[1], cells[group - 1], here, totals
    )
    arrived = returned[0] if group == 2 else jnp.concatenate(returned)
    return place_terms(base, there, arrived), collision


def solution(mesh):
    in_specs = (P(None, ("space", "mode")), P("mode", None, None), P(), P(), P())
    out_specs = (P(None, ("space", "mode")), P("mode", "space"))
    return jax.shard_map(shards, mesh=mesh, in_specs=in_specs, out_specs=out_specs, check_vma=False)
```

```python
import functools

import jax
import jax.numpy as jnp
from jax import lax
from jax.experimental import pallas as pl
from jax.experimental.pallas import tpu as pltpu
from jax.sharding import PartitionSpec as P

CLASSES = 3

wave_bound = 5.2
courant = 0.09
collision_update = 0.1

BF16 = jnp.bfloat16
F32 = jnp.float32
I32 = jnp.int32
VMEM = pl.BlockSpec(memory_space=pltpu.VMEM)
SMEM = pl.BlockSpec(memory_space=pltpu.SMEM)
HBM = pl.BlockSpec(memory_space=pltpu.HBM)
PARAMS = pltpu.CompilerParams(vmem_limit_bytes=16 * 2**20)


def remain(x):
    return pltpu.with_memory_space_constraint(x, pltpu.HBM)


def dot(a, b):
    return jnp.dot(a, b, preferred_element_type=F32)


def dot_general(a, b, da, db):
    return lax.dot_general(a, b, (((da,), (db,)), ((), ())), preferred_element_type=F32)


def halves(x):
    high = x.astype(BF16)
    return high, (x - high.astype(F32)).astype(BF16)


def iota(shape, axis):
    return lax.broadcasted_iota(I32, shape, axis)


def layout(rows, columns):
    cut = 5 * rows // 8 // 128 * 128
    tail = -(-(rows - cut) // 16) * 16
    lines = -(-rows // columns // 8) * 8
    return cut, tail, lines


def coarsen_kernel(state_hbm, *refs):
    small_hbm, head_ref, tail_ref, state_ref, small, sems = refs[:3], refs[3], refs[4], refs[5], refs[6:9], refs[9]
    rows, cut = state_ref.shape[0], head_ref.shape[0]
    parts = pl.ds(0, cut), pl.ds(cut, rows - cut)
    copies = [
        pltpu.make_async_copy(state_hbm.at[part], state_ref.at[part], sems.at[j])
        for j, part in enumerate(parts)
    ]
    copies += [
        pltpu.make_async_copy(source, target, sems.at[len(parts) + j])
        for j, (source, target) in enumerate(zip(small_hbm, small))
    ]
    for copy in copies:
        copy.start()
    copies[0].wait()
    head_ref[...] = state_ref[parts[0]].astype(BF16)
    copies[1].wait()
    tail = state_ref[parts[1]]
    tail_ref[...] = jnp.concatenate([tail, jnp.zeros((tail_ref.shape[0] - tail.shape[0], tail.shape[1]), F32)]).astype(BF16)
    for copy in copies[len(parts) :]:
        copy.wait()


def coarsen(state, table, thermal, target):
    rows, columns = state.shape
    cut, tail, lines = layout(rows, columns)
    return pl.pallas_call(
        coarsen_kernel,
        in_specs=[HBM] * 4,
        out_shape=(
            pltpu.VMEM((cut, columns), BF16),
            pltpu.VMEM((tail + 2 * lines, columns), BF16),
            pltpu.VMEM(state.shape, F32),
            pltpu.VMEM(table.shape, I32),
            pltpu.SMEM(thermal.shape, F32),
            pltpu.SMEM(target.shape, I32),
        ),
        out_specs=(VMEM, VMEM, VMEM, VMEM, SMEM, SMEM),
        scratch_shapes=[pltpu.SemaphoreType.DMA((5,))],
        compiler_params=PARAMS,
        name="coarsen",
    )(*(remain(x) for x in (state, table, thermal, target)))


def edges_kernel(head_ref, given_ref, tail_ref, ring_ref):
    cut, columns = head_ref.shape
    lines = ring_ref.shape[0]
    tail = tail_ref.shape[0] - 2 * lines
    rest = given_ref[0:tail]
    tail_ref[0:tail] = rest
    line, lane = iota((8, columns), 0), iota((8, columns), 1)
    pick = jnp.logical_or(
        jnp.logical_and(line == 0, lane == 0), jnp.logical_and(line == 1, lane == columns - 1)
    ).astype(BF16)
    found = jnp.concatenate([dot_general(pick, part, 1, 1) for part in (head_ref[...], rest)], axis=1)
    width = lines * columns
    found = jnp.concatenate([found, jnp.zeros((8, width - found.shape[1]), F32)], axis=1)
    folded = [
        jnp.concatenate([found[end : end + 1, j * columns : (j + 1) * columns] for j in range(lines)])
        for end in range(2)
    ]
    tail_ref[tail:] = jnp.concatenate(folded).astype(BF16)
    ring_ref[...] = jnp.where(lax.axis_index("mode") == 0, folded[0], folded[1]).astype(BF16)


def edges(rows, head, tail):
    columns = head.shape[1]
    return pl.pallas_call(
        edges_kernel,
        in_specs=[VMEM] * 2,
        out_shape=(pltpu.VMEM(tail.shape, BF16), pltpu.VMEM((layout(rows, columns)[2], columns), BF16)),
        out_specs=(VMEM,) * 2,
        compiler_params=PARAMS,
        name="edges",
    )(head, tail)


def advection_halves(table_ref, high_ref, low_ref):
    modes = table_ref.shape[1]
    index = [table_ref[j : j + 1, :].astype(F32) for j in range(3)]
    row = iota((8, modes), 0)
    weighted = jnp.where(row == 0, 144.0 * index[0], jnp.where(row == 1, 12.0 * index[1], index[2]))
    weighted = jnp.where(row < 3, weighted, 0.0).astype(BF16)
    along = jnp.where(row == 0, index[0], 0.0).astype(BF16)
    ones = jnp.ones((8, modes), BF16)
    code_down = dot_general(weighted, ones, 0, 0)
    along_down = dot_general(along, ones, 0, 0)
    code_across = 144.0 * index[0] + 12.0 * index[1] + index[2]
    matrix = jnp.where(code_across == code_down - 144.0, jnp.sqrt(along_down), 0.0)
    matrix = matrix + jnp.where(code_across == code_down + 144.0, jnp.sqrt(along_down + 1.0), 0.0)
    high_ref[...], low_ref[...] = halves(matrix)


def inner_transport(state_ref, high_ref, low_ref, thermal_ref, out_ref, diff_ref):
    rows, columns = state_ref.shape
    modes = high_ref.shape[0]
    state = state_ref[...]
    lane = iota((rows, columns), 1)
    before = jnp.where(lane == 0, 0.0, pltpu.roll(state, 1, 1))
    after = jnp.where(lane == columns - 1, 0.0, pltpu.roll(state, columns - 1, 1))
    diff_ref[...] = after - before
    out_ref[...] = before + after - 2.0 * state
    for c in range(CLASSES):
        part = pl.ds(c * modes, modes)
        d_high, d_low = halves(diff_ref[part])
        moved = dot(high_ref[...], d_high) + dot(high_ref[...], d_low) + dot(low_ref[...], d_high)
        diffused = (0.5 * wave_bound * courant) * out_ref[part]
        out_ref[part] = state_ref[part] + thermal_ref[c] * (diffused - (0.5 * courant) * moved)


def prepare(state_ref, table_ref, thermal_ref, tensor_hbm, outs, diff_ref, sem):
    tensor_ref, high_ref, low_ref, inner_ref = outs
    copy = pltpu.make_async_copy(tensor_hbm, tensor_ref, sem)
    copy.start()
    advection_halves(table_ref, high_ref, low_ref)
    inner_transport(state_ref, high_ref, low_ref, thermal_ref, inner_ref, diff_ref)
    copy.wait()


def at_seam():
    return jnp.logical_and(lax.axis_index("space") == 0, lax.axis_index("mode") == 0)


def early_kernel(ring_ref, state_ref, table_ref, thermal_ref, tensor_hbm, sent_ref, *refs):
    sent_ref[...] = ring_ref[...]

    @pl.when(at_seam())
    def _():
        prepare(state_ref, table_ref, thermal_ref, tensor_hbm, refs[:4], *refs[4:])


def late_kernel(state_ref, table_ref, thermal_ref, tensor_hbm, *refs):
    @pl.when(jnp.logical_not(at_seam()))
    def _():
        prepare(state_ref, table_ref, thermal_ref, tensor_hbm, refs[4:8], *refs[8:])


def held_shapes(tensor, state, modes):
    return (
        pltpu.VMEM(tensor.shape, BF16),
        pltpu.VMEM((modes, modes), BF16),
        pltpu.VMEM((modes, modes), BF16),
        pltpu.VMEM(state.shape, F32),
    )


def early(ring, state, table, thermal, tensor):
    shapes = (pltpu.VMEM(ring.shape, BF16),) + held_shapes(tensor, state, table.shape[1])
    return pl.pallas_call(
        early_kernel,
        in_specs=[VMEM, VMEM, VMEM, SMEM, HBM],
        out_shape=shapes,
        out_specs=(VMEM,) * len(shapes),
        scratch_shapes=[pltpu.VMEM(state.shape, F32), pltpu.SemaphoreType.DMA],
        compiler_params=PARAMS,
        name="early_prepare",
    )(ring, state, table, thermal, tensor)


def late(state, table, thermal, tensor, held):
    shapes = held_shapes(tensor, state, table.shape[1])
    return pl.pallas_call(
        late_kernel,
        in_specs=[VMEM, VMEM, SMEM, HBM] + [VMEM] * len(held),
        out_shape=shapes,
        out_specs=(VMEM,) * len(shapes),
        scratch_shapes=[pltpu.VMEM(state.shape, F32), pltpu.SemaphoreType.DMA],
        input_output_aliases={4 + j: j for j in range(len(held))},
        compiler_params=PARAMS,
        name="late_prepare",
    )(state, table, thermal, tensor, *held)


def classes(target_ref, first, shape, modes):
    line = iota(shape, 0)
    kind = jnp.zeros(shape, I32)
    for j in range(shape[0]):
        target = target_ref[first + j]
        own_class = sum((target >= c * modes).astype(I32) for c in range(1, CLASSES))
        kind = jnp.where(line == j, own_class, kind)
    return kind


def first_missing(cut, modes, c):
    return min(modes, max(0, cut - c * modes))


def begin_kernel(sets, target_ref, tensor_ref, *refs):
    heads, outs = refs[:sets], refs[sets:]
    cut, columns = heads[0].shape
    for at in range(0, sets, 2):
        sums_ref, product_ref, first_ref, wide_ref = *outs[at // 2 * 3 : at // 2 * 3 + 3], refs[-1]
        pair = range(at, min(at + 2, sets))
        shape = sums_ref.shape
        terms = shape[0]
        modes = tensor_ref.shape[0] // terms
        kind = classes(target_ref, lax.axis_index("mode") * terms, shape, modes)
        for j in pair:
            wide_ref[:, (j - at) * columns : (j - at + 1) * columns] = heads[j][...].astype(F32)
        cells = jnp.concatenate([heads[j][...] for j in pair], axis=1)
        product = dot(tensor_ref[:, 0:cut], cells).reshape(modes, *shape)
        missing = [first_missing(cut, modes, c) for c in range(CLASSES)]
        sums = [jnp.zeros(shape, F32) for _ in range(2)]
        for i in range(modes):
            first = jnp.zeros(shape, F32)
            later = jnp.zeros(shape, F32)
            for c in range(CLASSES):
                if i < missing[c]:
                    row = jnp.broadcast_to(wide_ref[pl.ds(c * modes + i, 1), 0 : shape[1]], shape)
                    first = row if c == 0 else jnp.where(kind == c, row, first)
                else:
                    first = jnp.where(kind == c, 0.0, first)
                    later = jnp.where(kind == c, product[i], later)
            first_ref[pl.ds(i * terms, terms)] = first
            if i >= min(missing):
                product_ref[pl.ds((i - min(missing)) * terms, terms)] = later
            sums[i % 2] = sums[i % 2] + first * product[i]
        sums_ref[...] = sums[0] + sums[1]


def begin(target, tensor, modes, heads):
    cut, columns = heads[0].shape
    terms = tensor.shape[0] // modes
    missing = min(first_missing(cut, modes, c) for c in range(CLASSES))
    shapes = []
    for at in range(0, len(heads), 2):
        width = columns * len(heads[at : at + 2])
        lengths = terms, (modes - missing) * terms, modes * terms
        shapes += [pltpu.VMEM((length, width), F32) for length in lengths]
    return pl.pallas_call(
        functools.partial(begin_kernel, len(heads)),
        in_specs=[SMEM, VMEM] + [VMEM] * len(heads),
        out_shape=tuple(shapes),
        out_specs=(VMEM,) * len(shapes),
        scratch_shapes=[pltpu.VMEM((cut, 2 * columns), F32)],
        compiler_params=PARAMS,
        name="begin_collide",
    )(target, tensor, *heads)


def finish_kernel(sets, target_ref, tensor_ref, *refs):
    begun, refs = refs[: (sets + 1) // 2 * 3], refs[(sets + 1) // 2 * 3 :]
    tails, totals, sent, wide_ref = refs[:sets], refs[sets : 2 * sets], refs[2 * sets : -1], refs[-1]
    terms, columns = totals[0].shape
    modes = tensor_ref.shape[0] // terms
    rows, rest = tensor_ref.shape[1], wide_ref.shape[0]
    cut = rows - rest
    missing = [first_missing(cut, modes, c) for c in range(CLASSES)]
    for at in range(0, sets, 2):
        sums_ref, product_ref, first_ref = begun[at // 2 * 3 : at // 2 * 3 + 3]
        pair = range(at, min(at + 2, sets))
        shape = sums_ref.shape
        kind = classes(target_ref, lax.axis_index("mode") * terms, shape, modes)
        parts = [tails[j][0:rest] for j in pair]
        for j, part in enumerate(parts):
            wide_ref[:, j * columns : (j + 1) * columns] = part.astype(F32)
        product = dot(tensor_ref[:, cut:], jnp.concatenate(parts, axis=1)).reshape(modes, *shape)
        sums = [sums_ref[...], jnp.zeros(shape, F32)]
        for i in range(modes):
            first = first_ref[pl.ds(i * terms, terms)]
            whole = product[i]
            for c in range(CLASSES):
                if i >= missing[c]:
                    row = jnp.broadcast_to(wide_ref[pl.ds(c * modes + i - cut, 1), 0 : shape[1]], shape)
                    first = jnp.where(kind == c, row, first)
            if i >= min(missing):
                whole = whole + product_ref[pl.ds((i - min(missing)) * terms, terms)]
            sums[i % 2] = sums[i % 2] + first * whole
        total = sums[0] + sums[1]
        for j in pair:
            part = total[:, (j - at) * columns : (j - at + 1) * columns]
            totals[j][...] = part
            if j > 0:
                sent[j - 1][...] = part.astype(BF16)


def finish(target, tensor, modes, begun, tails):
    sets = len(tails)
    rows, columns = tensor.shape[1], tails[0].shape[1]
    terms = tensor.shape[0] // modes
    shapes = [pltpu.VMEM((terms, columns), F32)] * sets + [pltpu.VMEM((terms, columns), BF16)] * (sets - 1)
    found = pl.pallas_call(
        functools.partial(finish_kernel, sets),
        in_specs=[SMEM, VMEM] + [VMEM] * (len(begun) + sets),
        out_shape=tuple(shapes),
        out_specs=(VMEM,) * len(shapes),
        scratch_shapes=[pltpu.VMEM((rows - layout(rows, columns)[0], 2 * columns), F32)],
        compiler_params=PARAMS,
        name="finish_collide",
    )(target, tensor, *begun, *tails)
    return found[:sets], found[sets:]


def ends_kernel(target_ref, thermal_ref, inner_ref, high_ref, low_ref, ring_ref, left_ref, right_ref, *refs):
    totals, base_ref, collision_ref = refs[:-2], *refs[-2:]
    rows, columns = inner_ref.shape
    modes = high_ref.shape[0]
    lines = ring_ref.shape[0]
    me, group = lax.axis_index("mode"), lax.axis_size("mode")
    terms = totals[0].shape[0]
    for r, terms_ref in enumerate(totals):
        start = pl.multiple_of(lax.rem(me + group - r, group) * columns, columns)
        collision_ref[:, pl.ds(start, columns)] = terms_ref[...]
    for j in range(terms):
        row = pl.ds(target_ref[me * terms + j], 1)
        base_ref[row] = base_ref[row] + collision_update * totals[0][j : j + 1]
    tail = left_ref.shape[0] - 2 * lines
    ring = ring_ref[...].astype(F32)
    left = jnp.where(me == 0, ring, left_ref[tail + lines : tail + 2 * lines].astype(F32))
    right = jnp.where(me == group - 1, ring, right_ref[tail : tail + lines].astype(F32))
    ends_of = [
        jnp.concatenate([folded[j : j + 1] for j in range(-(-rows // columns))], axis=1) for folded in (left, right)
    ]
    line = iota((8, modes), 0)
    packed = jnp.zeros((8, modes), F32)
    for c in range(CLASSES):
        for side, end in enumerate(ends_of):
            packed = jnp.where(line == 2 * c + side, end[:, c * modes : (c + 1) * modes], packed)
    coarse = packed.astype(BF16)
    moved = dot_general(high_ref[...], coarse, 1, 1) + dot_general(low_ref[...], coarse, 1, 1)
    lane = iota((1, 8), 1)
    speed = jnp.zeros((1, 8), F32)
    for c in range(CLASSES):
        speed = jnp.where(lane // 2 == c, thermal_ref[c], speed)
    sign = jnp.where(lane % 2 == 0, 1.0, -1.0)
    added = (0.5 * wave_bound * courant) * speed * packed.T + (0.5 * courant) * (sign * speed) * moved
    lane = iota((modes, columns), 1)
    for c in range(CLASSES):
        part = pl.ds(c * modes, modes)
        first = jnp.broadcast_to(added[:, 2 * c : 2 * c + 1], (modes, columns))
        last = jnp.broadcast_to(added[:, 2 * c + 1 : 2 * c + 2], (modes, columns))
        base_ref[part] = base_ref[part] + jnp.where(lane == 0, first, jnp.where(lane == columns - 1, last, 0.0))


def ends(target, thermal, inner, high, low, ring, left, right, totals):
    terms, columns = totals[0].shape
    return pl.pallas_call(
        ends_kernel,
        in_specs=[SMEM, SMEM] + [VMEM] * (6 + len(totals)),
        out_shape=(
            pltpu.VMEM(inner.shape, F32),
            pltpu.VMEM((terms, len(totals) * columns), F32),
        ),
        out_specs=(VMEM, VMEM),
        input_output_aliases={2: 0},
        compiler_params=PARAMS,
        name="ends",
    )(target, thermal, inner, high, low, ring, left, right, *totals)


def place_kernel(target_ref, _, *refs):
    arrived, (collision_ref, base_ref, out_hbm, collision_hbm, sems) = refs[:-5], refs[-5:]
    terms = arrived[0].shape[0]
    me, group = lax.axis_index("mode"), lax.axis_size("mode")
    copies = [pltpu.make_async_copy(collision_ref, collision_hbm, sems.at[0])]
    copies[0].start()
    for r, terms_ref in enumerate(arrived, 1):
        first = lax.rem(me + r, group) * terms
        values = collision_update * terms_ref[...].astype(F32)
        for j in range(terms):
            row = pl.ds(target_ref[first + j], 1)
            base_ref[row] = base_ref[row] + values[j : j + 1]
    copies.append(pltpu.make_async_copy(base_ref, out_hbm, sems.at[1]))
    copies[1].start()
    for copy in copies:
        copy.wait()


def place(target, base, arrived, collision):
    return pl.pallas_call(
        place_kernel,
        in_specs=[SMEM, VMEM] + [VMEM] * (len(arrived) + 1),
        out_shape=(
            pltpu.VMEM(base.shape, F32),
            jax.ShapeDtypeStruct(base.shape, F32),
            jax.ShapeDtypeStruct(collision.shape, F32),
        ),
        out_specs=(VMEM, HBM, HBM),
        scratch_shapes=[pltpu.SemaphoreType.DMA((2,))],
        input_output_aliases={1: 0},
        compiler_params=PARAMS,
        name="place",
    )(target, base, *arrived, collision)


def shards(state, tensor, table, thermal, output_mode_row):
    rows = state.shape[0]
    terms, modes, _ = tensor.shape
    slabs, group = lax.axis_size("space"), lax.axis_size("mode")

    def shift(x, by):
        return lax.ppermute(x, "mode", [(i, (i + by) % group) for i in range(group)])

    head, tail, wide, index, speed, target = coarsen(state, table.T, thermal, output_mode_row)
    heads = [head] + [shift(head, r) for r in range(1, group)]
    tail, ring = edges(rows, head, tail)
    tails = [tail] + [shift(tail, r) for r in range(1, group)]

    flat = remain(jnp.transpose(tensor, (1, 0, 2)).reshape(modes * terms, rows))
    ring, *held = early(ring, wide, index, speed, flat)
    size = slabs * group
    pairs = [(s * group + group - 1, (s + 1) * group % size) for s in range(slabs)]
    ring = lax.ppermute(ring, ("space", "mode"), pairs + [(j, i) for i, j in pairs])
    held_tensor, high, low, inner = late(wide, index, speed, flat, held)

    begun = begin(target, held_tensor, modes, heads)
    totals, sent = finish(target, held_tensor, modes, begun, tails)
    arrived = [shift(x, group - r) for r, x in enumerate(sent, 1)]
    base, collision = ends(target, speed, inner, high, low, ring, tails[1], tails[group - 1], totals)
    return place(target, base, arrived, collision)[1:]


def solution(mesh):
    in_specs = (P(None, ("space", "mode")), P("mode", None, None), P(), P(), P())
    out_specs = (P(None, ("space", "mode")), P("mode", "space"))
    return jax.shard_map(shards, mesh=mesh, in_specs=in_specs, out_specs=out_specs, check_vma=False)
```

```python
import jax
import jax.numpy as jnp
from jax import lax
from jax.experimental import pallas as pl
from jax.experimental.pallas import tpu as pltpu
from jax.sharding import PartitionSpec as P

CLASSES = 3

wave_bound = 5.2
courant = 0.09
collision_update = 0.1

BF16 = jnp.bfloat16
F32 = jnp.float32
I32 = jnp.int32
VMEM = pl.BlockSpec(memory_space=pltpu.VMEM)
SMEM = pl.BlockSpec(memory_space=pltpu.SMEM)
HBM = pl.BlockSpec(memory_space=pltpu.HBM)
PARAMS = pltpu.CompilerParams(vmem_limit_bytes=16 * 2**20)


def remain(x):
    return pltpu.with_memory_space_constraint(x, pltpu.HBM)


def dot(a, b):
    return jnp.dot(a, b, preferred_element_type=F32)


def dot_general(a, b, da, db):
    return lax.dot_general(a, b, (((da,), (db,)), ((), ())), preferred_element_type=F32)


def halves(x):
    high = x.astype(BF16)
    return high, (x - high.astype(F32)).astype(BF16)


def iota(shape, axis):
    return lax.broadcasted_iota(I32, shape, axis)


def coarsen_kernel(state_hbm, *refs):
    small_hbm, coarse_ref, state_ref, small, sems = refs[:3], refs[3], refs[4], refs[5:8], refs[8]
    rows = state_ref.shape[0]
    cut = rows // 2 // 16 * 16
    parts = pl.ds(0, cut), pl.ds(cut, rows - cut)
    copies = [
        pltpu.make_async_copy(state_hbm.at[part], state_ref.at[part], sems.at[j])
        for j, part in enumerate(parts)
    ]
    copies += [
        pltpu.make_async_copy(source, target, sems.at[len(parts) + j])
        for j, (source, target) in enumerate(zip(small_hbm, small))
    ]
    for copy in copies:
        copy.start()
    for part, copy in zip(parts, copies):
        copy.wait()
        coarse_ref[part] = state_ref[part].astype(BF16)
    for copy in copies[len(parts) :]:
        copy.wait()


def coarsen(state, table, thermal, target):
    return pl.pallas_call(
        coarsen_kernel,
        in_specs=[HBM] * 4,
        out_shape=(
            pltpu.VMEM(state.shape, BF16),
            pltpu.VMEM(state.shape, F32),
            pltpu.VMEM(table.shape, I32),
            pltpu.SMEM(thermal.shape, F32),
            pltpu.SMEM(target.shape, I32),
        ),
        out_specs=(VMEM, VMEM, VMEM, SMEM, SMEM),
        scratch_shapes=[pltpu.SemaphoreType.DMA((5,))],
        compiler_params=PARAMS,
        name="coarsen",
    )(*(remain(x) for x in (state, table, thermal, target)))


def advection_halves(table_ref, high_ref, low_ref):
    modes = table_ref.shape[1]
    index = [table_ref[j : j + 1, :].astype(F32) for j in range(3)]
    row = iota((8, modes), 0)
    weighted = jnp.where(row == 0, 144.0 * index[0], jnp.where(row == 1, 12.0 * index[1], index[2]))
    weighted = jnp.where(row < 3, weighted, 0.0).astype(BF16)
    along = jnp.where(row == 0, index[0], 0.0).astype(BF16)
    ones = jnp.ones((8, modes), BF16)
    code_down = dot_general(weighted, ones, 0, 0)
    along_down = dot_general(along, ones, 0, 0)
    code_across = 144.0 * index[0] + 12.0 * index[1] + index[2]
    matrix = jnp.where(code_across == code_down - 144.0, jnp.sqrt(along_down), 0.0)
    matrix = matrix + jnp.where(code_across == code_down + 144.0, jnp.sqrt(along_down + 1.0), 0.0)
    high_ref[...], low_ref[...] = halves(matrix)


def inner_transport(state_ref, high_ref, low_ref, thermal_ref, out_ref, diff_ref):
    rows, columns = state_ref.shape
    modes = high_ref.shape[0]
    state = state_ref[...]
    lane = iota((rows, columns), 1)
    before = jnp.where(lane == 0, 0.0, pltpu.roll(state, 1, 1))
    after = jnp.where(lane == columns - 1, 0.0, pltpu.roll(state, columns - 1, 1))
    diff_ref[...] = after - before
    out_ref[...] = before + after - 2.0 * state
    for c in range(CLASSES):
        part = pl.ds(c * modes, modes)
        d_high, d_low = halves(diff_ref[part])
        moved = dot(high_ref[...], d_high) + dot(high_ref[...], d_low) + dot(low_ref[...], d_high)
        diffused = (0.5 * wave_bound * courant) * out_ref[part]
        out_ref[part] = state_ref[part] + thermal_ref[c] * (diffused - (0.5 * courant) * moved)


def prepare(state_ref, table_ref, thermal_ref, target_ref, tensor_hbm, outs, diff_ref, sem):
    tensor_ref, high_ref, low_ref, inner_ref, kind_ref, own_ref = outs
    copy = pltpu.make_async_copy(tensor_hbm, tensor_ref, sem)
    modes = high_ref.shape[0]
    kind_ref[...] = classes(target_ref, lax.axis_index("mode") * kind_ref.shape[0], kind_ref.shape, modes)
    own_ref[...] = state_ref[...].astype(BF16).astype(F32)
    copy.start()
    advection_halves(table_ref, high_ref, low_ref)
    inner_transport(state_ref, high_ref, low_ref, thermal_ref, inner_ref, diff_ref)
    copy.wait()


FIRST, EARLY, LATE = range(3)


def stage():
    slab = lax.axis_index("space")
    return jnp.where(slab == 1, FIRST, jnp.where(slab == 0, EARLY, LATE))


def first_kernel(state_ref, table_ref, thermal_ref, target_ref, tensor_hbm, coarse_ref, *refs):
    @pl.when(stage() == FIRST)
    def _():
        prepare(state_ref, table_ref, thermal_ref, target_ref, tensor_hbm, refs[1:7], *refs[7:])


def early_kernel(state_ref, table_ref, thermal_ref, target_ref, tensor_hbm, coarse_ref, *refs):
    rows, columns = coarse_ref.shape
    edge_ref, refs = refs[6], refs[7:]
    wanted = jnp.where(lax.axis_index("mode") == 0, 0, columns - 1)
    pick = (iota((8, columns), 1) == wanted).astype(BF16)
    edge = dot_general(pick, coarse_ref[...], 1, 1)
    lines = edge_ref.shape[0]
    edge = jnp.concatenate([edge, jnp.zeros((8, lines * columns - rows), F32)], axis=1)
    folded = [edge[0:1, j * columns : (j + 1) * columns] for j in range(lines)]
    edge_ref[...] = jnp.concatenate(folded).astype(BF16)

    @pl.when(stage() == EARLY)
    def _():
        prepare(state_ref, table_ref, thermal_ref, target_ref, tensor_hbm, refs[:6], *refs[6:])


def late_kernel(state_ref, table_ref, thermal_ref, target_ref, tensor_hbm, *refs):
    @pl.when(stage() == LATE)
    def _():
        prepare(state_ref, table_ref, thermal_ref, target_ref, tensor_hbm, refs[6:12], *refs[12:])


def held_shapes(tensor, state, modes):
    return (
        pltpu.VMEM(tensor.shape, BF16),
        pltpu.VMEM((modes, modes), BF16),
        pltpu.VMEM((modes, modes), BF16),
        pltpu.VMEM(state.shape, F32),
        pltpu.VMEM((tensor.shape[0] // modes, 2 * state.shape[1]), I32),
        pltpu.VMEM(state.shape, F32),
    )


def preparing(kernel, state, table, thermal, target, tensor, coarse=None, held=None, extra=()):
    shapes = held_shapes(tensor, state, table.shape[1])
    given = [x for x in (coarse,) if x is not None] + list(held or ())
    inputs = 5 + (coarse is not None)
    aliases = {inputs + j: len(extra) + j for j in range(len(held or ()))}
    if kernel is first_kernel:
        aliases = {5: 0}
    return pl.pallas_call(
        kernel,
        in_specs=[VMEM, VMEM, SMEM, SMEM, HBM] + [VMEM] * len(given),
        out_shape=tuple(extra) + shapes,
        out_specs=(VMEM,) * (len(extra) + len(shapes)),
        scratch_shapes=[pltpu.VMEM(state.shape, F32), pltpu.SemaphoreType.DMA],
        input_output_aliases=aliases,
        compiler_params=PARAMS,
        name=kernel.__name__,
    )(state, table, thermal, target, tensor, *given)


def classes(target_ref, first, shape, modes):
    line = iota(shape, 0)
    kind = jnp.zeros(shape, I32)
    for j in range(shape[0]):
        target = target_ref[first + j]
        own_class = sum((target >= c * modes).astype(I32) for c in range(1, CLASSES))
        kind = jnp.where(line == j, own_class, kind)
    return kind


def contract(tensor_ref, cells, wide, kind):
    terms, columns = kind.shape
    modes = tensor_ref.shape[0] // terms
    product = dot(tensor_ref[...], cells).reshape(modes, terms, columns)
    sums = [jnp.zeros((terms, columns), F32) for _ in range(2)]

    def row(j):
        rows = [jnp.broadcast_to(ref[pl.ds(j, 1)], (terms, ref.shape[1])) for ref in wide]
        return jnp.concatenate(rows, axis=1)

    for i in range(modes):
        first = row(i)
        for c in range(1, CLASSES):
            first = jnp.where(kind == c, row(c * modes + i), first)
        sums[i % 2] = sums[i % 2] + first * product[i]
    return sums[0] + sums[1]


def collide_kernel(tensor_ref, kind_ref, own_ref, *refs):
    sets = len(refs) // 3
    given, totals, sent, wide_refs = refs[:sets], refs[sets : 2 * sets], refs[2 * sets : -1], refs[-1]
    columns = totals[0].shape[1]
    for at in range(0, sets, 2):
        pair = given[at : at + 2]
        cells = jnp.concatenate([ref[...] for ref in pair], axis=1)
        wide = []
        for j, ref in enumerate(pair):
            if at + j == 0:
                wide.append(own_ref)
            else:
                wide.append(wide_refs.at[j])
                wide_refs[j] = ref[...].astype(F32)
        total = contract(tensor_ref, cells, wide, kind_ref[:, 0 : len(pair) * columns])
        for j in range(len(pair)):
            part = total[:, j * columns : (j + 1) * columns]
            totals[at + j][...] = part
            if at + j > 0:
                sent[at + j - 1][...] = part.astype(BF16)


def collide(tensor, kind, own, cells):
    sets = len(cells)
    columns = cells[0].shape[1]
    terms = kind.shape[0]
    shapes = [pltpu.VMEM((terms, columns), F32)] * sets + [pltpu.VMEM((terms, columns), BF16)] * (sets - 1)
    found = pl.pallas_call(
        collide_kernel,
        in_specs=[VMEM] * (3 + sets),
        out_shape=tuple(shapes),
        out_specs=(VMEM,) * len(shapes),
        scratch_shapes=[pltpu.VMEM((2, *own.shape), F32)],
        compiler_params=PARAMS,
        name="collide",
    )(tensor, kind, own, *cells)
    return found[:sets], found[sets:]


def ends_kernel(target_ref, thermal_ref, inner_ref, high_ref, low_ref, ring_ref, left_ref, right_ref, *refs):
    totals, base_ref, collision_ref = refs[:-2], *refs[-2:]
    rows, columns = inner_ref.shape
    modes = high_ref.shape[0]
    me, group = lax.axis_index("mode"), lax.axis_size("mode")
    terms = totals[0].shape[0]
    for r, terms_ref in enumerate(totals):
        start = pl.multiple_of(lax.rem(me + group - r, group) * columns, columns)
        collision_ref[:, pl.ds(start, columns)] = terms_ref[...]
    for j in range(terms):
        row = pl.ds(target_ref[me * terms + j], 1)
        base_ref[row] = base_ref[row] + collision_update * totals[0][j : j + 1]
    line, lane = iota((8, columns), 0), iota((8, columns), 1)
    last = jnp.logical_and(line == 0, lane == columns - 1)
    first = jnp.logical_and(line == 1, lane == 0)
    if group == 2:
        beyond = dot_general(jnp.logical_or(last, first).astype(BF16), left_ref[...], 1, 1)
    else:
        beyond = dot_general(last.astype(BF16), left_ref[...], 1, 1)
        beyond = beyond + dot_general(first.astype(BF16), right_ref[...], 1, 1)
    ring = ring_ref[...].astype(F32)
    ring = jnp.concatenate([ring[j : j + 1] for j in range(-(-rows // columns))], axis=1)[:, 0:rows]
    ends_of = jnp.where(me == 0, ring, beyond[0:1]), jnp.where(me == group - 1, ring, beyond[1:2])
    line = iota((8, modes), 0)
    packed = jnp.zeros((8, modes), F32)
    for c in range(CLASSES):
        for side, end in enumerate(ends_of):
            packed = jnp.where(line == 2 * c + side, end[:, c * modes : (c + 1) * modes], packed)
    coarse = packed.astype(BF16)
    moved = dot_general(high_ref[...], coarse, 1, 1) + dot_general(low_ref[...], coarse, 1, 1)
    lane = iota((1, 8), 1)
    speed = jnp.zeros((1, 8), F32)
    for c in range(CLASSES):
        speed = jnp.where(lane // 2 == c, thermal_ref[c], speed)
    sign = jnp.where(lane % 2 == 0, 1.0, -1.0)
    added = (0.5 * wave_bound * courant) * speed * packed.T + (0.5 * courant) * (sign * speed) * moved
    lane = iota((modes, columns), 1)
    for c in range(CLASSES):
        part = pl.ds(c * modes, modes)
        first = jnp.broadcast_to(added[:, 2 * c : 2 * c + 1], (modes, columns))
        last = jnp.broadcast_to(added[:, 2 * c + 1 : 2 * c + 2], (modes, columns))
        base_ref[part] = base_ref[part] + jnp.where(lane == 0, first, jnp.where(lane == columns - 1, last, 0.0))


def ends(target, thermal, inner, high, low, ring, left, right, totals):
    terms, columns = totals[0].shape
    return pl.pallas_call(
        ends_kernel,
        in_specs=[SMEM, SMEM] + [VMEM] * (6 + len(totals)),
        out_shape=(
            pltpu.VMEM(inner.shape, F32),
            pltpu.VMEM((terms, len(totals) * columns), F32),
        ),
        out_specs=(VMEM, VMEM),
        input_output_aliases={2: 0},
        compiler_params=PARAMS,
        name="ends",
    )(target, thermal, inner, high, low, ring, left, right, *totals)


def place_kernel(target_ref, _, *refs):
    arrived, (collision_ref, base_ref, out_hbm, collision_hbm, sems) = refs[:-5], refs[-5:]
    terms = arrived[0].shape[0]
    me, group = lax.axis_index("mode"), lax.axis_size("mode")
    copies = [pltpu.make_async_copy(collision_ref, collision_hbm, sems.at[0])]
    for r, terms_ref in enumerate(arrived, 1):
        first = lax.rem(me + r, group) * terms
        values = collision_update * terms_ref[...].astype(F32)
        for j in range(terms):
            row = pl.ds(target_ref[first + j], 1)
            base_ref[row] = base_ref[row] + values[j : j + 1]
    copies.append(pltpu.make_async_copy(base_ref, out_hbm, sems.at[1]))
    copies[1].start()
    copies[0].start()
    for copy in copies:
        copy.wait()


def place(target, base, arrived, collision):
    return pl.pallas_call(
        place_kernel,
        in_specs=[SMEM, VMEM] + [VMEM] * (len(arrived) + 1),
        out_shape=(
            pltpu.VMEM(base.shape, F32),
            jax.ShapeDtypeStruct(base.shape, F32),
            jax.ShapeDtypeStruct(collision.shape, F32),
        ),
        out_specs=(VMEM, HBM, HBM),
        scratch_shapes=[pltpu.SemaphoreType.DMA((2,))],
        input_output_aliases={1: 0},
        compiler_params=PARAMS,
        name="place",
    )(target, base, *arrived, collision)


def shards(state, tensor, table, thermal, output_mode_row):
    rows = state.shape[0]
    terms, modes, _ = tensor.shape
    slabs, group = lax.axis_size("space"), lax.axis_size("mode")

    def shift(x, by):
        return lax.ppermute(x, "mode", [(i, (i + by) % group) for i in range(group)])

    columns = state.shape[1]
    flat = remain(jnp.transpose(tensor, (1, 0, 2)).reshape(modes * terms, rows))
    coarse, wide, index, speed, target = coarsen(state, table.T, thermal, output_mode_row)
    given = wide, index, speed, target, flat
    coarse, *held = preparing(first_kernel, *given, coarse, extra=[pltpu.VMEM(coarse.shape, BF16)])
    cells = [coarse] + [shift(coarse, r) for r in range(1, group)]

    lines = -(-rows // columns // 8) * 8
    edge, *held = preparing(early_kernel, *given, coarse, held, extra=[pltpu.VMEM((lines, columns), BF16)])
    size = slabs * group
    pairs = [(s * group + group - 1, (s + 1) * group % size) for s in range(slabs)]
    ring = lax.ppermute(edge, ("space", "mode"), pairs + [(j, i) for i, j in pairs])
    held_tensor, high, low, inner, kind, own = preparing(late_kernel, *given, held=held)

    totals, sent = collide(held_tensor, kind, own, cells)
    arrived = [shift(x, group - r) for r, x in enumerate(sent, 1)]
    base, collision = ends(target, speed, inner, high, low, ring, cells[1], cells[group - 1], totals)
    return place(target, base, arrived, collision)[1:]


def solution(mesh):
    in_specs = (P(None, ("space", "mode")), P("mode", None, None), P(), P(), P())
    out_specs = (P(None, ("space", "mode")), P("mode", "space"))
    return jax.shard_map(shards, mesh=mesh, in_specs=in_specs, out_specs=out_specs, check_vma=False)
```

```python
import jax
import jax.numpy as jnp
from jax import lax
from jax.experimental import pallas as pl
from jax.experimental.pallas import tpu as pltpu
from jax.sharding import PartitionSpec as P

CLASSES = 3

wave_bound = 5.2
courant = 0.09
collision_update = 0.1

BF16 = jnp.bfloat16
F32 = jnp.float32
I32 = jnp.int32
VMEM = pl.BlockSpec(memory_space=pltpu.VMEM)
SMEM = pl.BlockSpec(memory_space=pltpu.SMEM)
HBM = pl.BlockSpec(memory_space=pltpu.HBM)
PARAMS = pltpu.CompilerParams(vmem_limit_bytes=16 * 2**20)


def remain(x):
    return pltpu.with_memory_space_constraint(x, pltpu.HBM)


def dot(a, b):
    return jnp.dot(a, b, preferred_element_type=F32)


def dot_general(a, b, da, db):
    return lax.dot_general(a, b, (((da,), (db,)), ((), ())), preferred_element_type=F32)


def halves(x):
    high = x.astype(BF16)
    return high, (x - high.astype(F32)).astype(BF16)


def iota(shape, axis):
    return lax.broadcasted_iota(I32, shape, axis)


def coarsen_kernel(state_hbm, *refs):
    small_hbm, tensor_hbm, coarse_ref, state_ref, small = refs[:3], refs[3], refs[4], refs[5], refs[6:9]
    outs, (sems, *scratch) = refs[9:15], refs[15:]
    rows = state_ref.shape[0]
    cut = rows // 2 // 16 * 16
    parts = pl.ds(0, cut), pl.ds(cut, rows - cut)
    copies = [
        pltpu.make_async_copy(state_hbm.at[part], state_ref.at[part], sems.at[j])
        for j, part in enumerate(parts)
    ]
    copies += [
        pltpu.make_async_copy(source, target, sems.at[len(parts) + j])
        for j, (source, target) in enumerate(zip(small_hbm, small))
    ]
    for copy in copies:
        copy.start()
    for part, copy in zip(parts, copies):
        copy.wait()
        coarse_ref[part] = state_ref[part].astype(BF16)
    for copy in copies[len(parts) :]:
        copy.wait()

    @pl.when(stage() == FIRST)
    def _():
        prepare(state_ref, *small, tensor_hbm, outs, *scratch)


def coarsen(state, table, thermal, target, tensor):
    shapes = (
        pltpu.VMEM(state.shape, BF16),
        pltpu.VMEM(state.shape, F32),
        pltpu.VMEM(table.shape, I32),
        pltpu.SMEM(thermal.shape, F32),
        pltpu.SMEM(target.shape, I32),
    )
    held = held_shapes(tensor, state, table.shape[1])
    return pl.pallas_call(
        coarsen_kernel,
        in_specs=[HBM] * 5,
        out_shape=shapes + held,
        out_specs=(VMEM, VMEM, VMEM, SMEM, SMEM) + (VMEM,) * len(held),
        scratch_shapes=[
            pltpu.SemaphoreType.DMA((5,)),
            pltpu.VMEM(state.shape, F32),
            pltpu.SemaphoreType.DMA,
        ],
        compiler_params=PARAMS,
        name="coarsen",
    )(*(remain(x) for x in (state, table, thermal, target)), tensor)


def advection_halves(table_ref, high_ref, low_ref):
    modes = table_ref.shape[1]
    index = [table_ref[j : j + 1, :].astype(F32) for j in range(3)]
    row = iota((8, modes), 0)
    weighted = jnp.where(row == 0, 144.0 * index[0], jnp.where(row == 1, 12.0 * index[1], index[2]))
    weighted = jnp.where(row < 3, weighted, 0.0).astype(BF16)
    along = jnp.where(row == 0, index[0], 0.0).astype(BF16)
    ones = jnp.ones((8, modes), BF16)
    code_down = dot_general(weighted, ones, 0, 0)
    along_down = dot_general(along, ones, 0, 0)
    code_across = 144.0 * index[0] + 12.0 * index[1] + index[2]
    matrix = jnp.where(code_across == code_down - 144.0, jnp.sqrt(along_down), 0.0)
    matrix = matrix + jnp.where(code_across == code_down + 144.0, jnp.sqrt(along_down + 1.0), 0.0)
    high_ref[...], low_ref[...] = halves(matrix)


def inner_transport(state_ref, high_ref, low_ref, thermal_ref, out_ref, diff_ref):
    rows, columns = state_ref.shape
    modes = high_ref.shape[0]
    state = state_ref[...]
    lane = iota((rows, columns), 1)
    before = jnp.where(lane == 0, 0.0, pltpu.roll(state, 1, 1))
    after = jnp.where(lane == columns - 1, 0.0, pltpu.roll(state, columns - 1, 1))
    diff_ref[...] = after - before
    out_ref[...] = before + after - 2.0 * state
    for c in range(CLASSES):
        part = pl.ds(c * modes, modes)
        d_high, d_low = halves(diff_ref[part])
        moved = dot(high_ref[...], d_high) + dot(high_ref[...], d_low) + dot(low_ref[...], d_high)
        diffused = (0.5 * wave_bound * courant) * out_ref[part]
        out_ref[part] = state_ref[part] + thermal_ref[c] * (diffused - (0.5 * courant) * moved)


def prepare(state_ref, table_ref, thermal_ref, target_ref, tensor_hbm, outs, diff_ref, sem):
    tensor_ref, high_ref, low_ref, inner_ref, kind_ref, own_ref = outs
    copy = pltpu.make_async_copy(tensor_hbm, tensor_ref, sem)
    modes = high_ref.shape[0]
    kind_ref[...] = classes(target_ref, lax.axis_index("mode") * kind_ref.shape[0], kind_ref.shape, modes)
    own_ref[...] = state_ref[...].astype(BF16).astype(F32)
    copy.start()
    advection_halves(table_ref, high_ref, low_ref)
    inner_transport(state_ref, high_ref, low_ref, thermal_ref, inner_ref, diff_ref)
    copy.wait()


FIRST, EARLY, LATE = range(3)


def stage():
    slab = lax.axis_index("space")
    return jnp.where(slab == 1, FIRST, jnp.where(slab == 0, EARLY, LATE))


def early_kernel(state_ref, table_ref, thermal_ref, target_ref, tensor_hbm, coarse_ref, *refs):
    rows, columns = coarse_ref.shape
    edge_ref, refs = refs[6], refs[7:]
    wanted = jnp.where(lax.axis_index("mode") == 0, 0, columns - 1)
    pick = (iota((8, columns), 1) == wanted).astype(BF16)
    edge = dot_general(pick, coarse_ref[...], 1, 1)
    lines = edge_ref.shape[0]
    edge = jnp.concatenate([edge, jnp.zeros((8, lines * columns - rows), F32)], axis=1)
    folded = [edge[0:1, j * columns : (j + 1) * columns] for j in range(lines)]
    edge_ref[...] = jnp.concatenate(folded).astype(BF16)

    @pl.when(stage() == EARLY)
    def _():
        prepare(state_ref, table_ref, thermal_ref, target_ref, tensor_hbm, refs[:6], *refs[6:])


def late_kernel(state_ref, table_ref, thermal_ref, target_ref, tensor_hbm, *refs):
    @pl.when(stage() == LATE)
    def _():
        prepare(state_ref, table_ref, thermal_ref, target_ref, tensor_hbm, refs[6:12], *refs[12:])


def held_shapes(tensor, state, modes):
    return (
        pltpu.VMEM(tensor.shape, BF16),
        pltpu.VMEM((modes, modes), BF16),
        pltpu.VMEM((modes, modes), BF16),
        pltpu.VMEM(state.shape, F32),
        pltpu.VMEM((tensor.shape[0] // modes, 2 * state.shape[1]), I32),
        pltpu.VMEM(state.shape, F32),
    )


def preparing(kernel, state, table, thermal, target, tensor, held, coarse=(), extra=()):
    shapes = tuple(extra) + held_shapes(tensor, state, table.shape[1])
    given = 5 + len(coarse)
    return pl.pallas_call(
        kernel,
        in_specs=[VMEM, VMEM, SMEM, SMEM, HBM] + [VMEM] * (len(coarse) + len(held)),
        out_shape=shapes,
        out_specs=(VMEM,) * len(shapes),
        scratch_shapes=[pltpu.VMEM(state.shape, F32), pltpu.SemaphoreType.DMA],
        input_output_aliases={given + j: len(extra) + j for j in range(len(held))},
        compiler_params=PARAMS,
        name=kernel.__name__,
    )(state, table, thermal, target, tensor, *coarse, *held)


def classes(target_ref, first, shape, modes):
    line = iota(shape, 0)
    kind = jnp.zeros(shape, I32)
    for j in range(shape[0]):
        target = target_ref[first + j]
        own_class = sum((target >= c * modes).astype(I32) for c in range(1, CLASSES))
        kind = jnp.where(line == j, own_class, kind)
    return kind


def contract(tensor_ref, cells, wide, kind):
    terms, columns = kind.shape
    modes = tensor_ref.shape[0] // terms
    product = dot(tensor_ref[...], cells).reshape(modes, terms, columns)
    sums = [jnp.zeros((terms, columns), F32) for _ in range(2)]

    def row(j):
        rows = [jnp.broadcast_to(ref[pl.ds(j, 1)], (terms, ref.shape[1])) for ref in wide]
        return jnp.concatenate(rows, axis=1)

    for i in range(modes):
        first = row(i)
        for c in range(1, CLASSES):
            first = jnp.where(kind == c, row(c * modes + i), first)
        sums[i % 2] = sums[i % 2] + first * product[i]
    return sums[0] + sums[1]


def collide_kernel(tensor_ref, kind_ref, own_ref, *refs):
    sets = len(refs) // 3
    given, totals, sent, wide_refs = refs[:sets], refs[sets : 2 * sets], refs[2 * sets : -1], refs[-1]
    columns = totals[0].shape[1]
    for at in range(0, sets, 2):
        pair = given[at : at + 2]
        cells = jnp.concatenate([ref[...] for ref in pair], axis=1)
        wide = []
        for j, ref in enumerate(pair):
            if at + j == 0:
                wide.append(own_ref)
            else:
                wide.append(wide_refs.at[j])
                wide_refs[j] = ref[...].astype(F32)
        total = contract(tensor_ref, cells, wide, kind_ref[:, 0 : len(pair) * columns])
        for j in range(len(pair)):
            part = total[:, j * columns : (j + 1) * columns]
            totals[at + j][...] = part
            if at + j > 0:
                sent[at + j - 1][...] = part.astype(BF16)


def collide(tensor, kind, own, cells):
    sets = len(cells)
    columns = cells[0].shape[1]
    terms = kind.shape[0]
    shapes = [pltpu.VMEM((terms, columns), F32)] * sets + [pltpu.VMEM((terms, columns), BF16)] * (sets - 1)
    found = pl.pallas_call(
        collide_kernel,
        in_specs=[VMEM] * (3 + sets),
        out_shape=tuple(shapes),
        out_specs=(VMEM,) * len(shapes),
        scratch_shapes=[pltpu.VMEM((2, *own.shape), F32)],
        compiler_params=PARAMS,
        name="collide",
    )(tensor, kind, own, *cells)
    return found[:sets], found[sets:]


def ends_kernel(target_ref, thermal_ref, inner_ref, high_ref, low_ref, ring_ref, left_ref, right_ref, *refs):
    totals, base_ref, collision_ref = refs[:-2], *refs[-2:]
    rows, columns = inner_ref.shape
    modes = high_ref.shape[0]
    me, group = lax.axis_index("mode"), lax.axis_size("mode")
    terms = totals[0].shape[0]
    for r, terms_ref in enumerate(totals):
        start = pl.multiple_of(lax.rem(me + group - r, group) * columns, columns)
        collision_ref[:, pl.ds(start, columns)] = terms_ref[...]
    for j in range(terms):
        row = pl.ds(target_ref[me * terms + j], 1)
        base_ref[row] = base_ref[row] + collision_update * totals[0][j : j + 1]
    line, lane = iota((8, columns), 0), iota((8, columns), 1)
    last = jnp.logical_and(line == 0, lane == columns - 1)
    first = jnp.logical_and(line == 1, lane == 0)
    if group == 2:
        beyond = dot_general(jnp.logical_or(last, first).astype(BF16), left_ref[...], 1, 1)
    else:
        beyond = dot_general(last.astype(BF16), left_ref[...], 1, 1)
        beyond = beyond + dot_general(first.astype(BF16), right_ref[...], 1, 1)
    ring = ring_ref[...].astype(F32)
    ring = jnp.concatenate([ring[j : j + 1] for j in range(-(-rows // columns))], axis=1)[:, 0:rows]
    ends_of = jnp.where(me == 0, ring, beyond[0:1]), jnp.where(me == group - 1, ring, beyond[1:2])
    line = iota((8, modes), 0)
    packed = jnp.zeros((8, modes), F32)
    for c in range(CLASSES):
        for side, end in enumerate(ends_of):
            packed = jnp.where(line == 2 * c + side, end[:, c * modes : (c + 1) * modes], packed)
    coarse = packed.astype(BF16)
    moved = dot_general(high_ref[...], coarse, 1, 1) + dot_general(low_ref[...], coarse, 1, 1)
    lane = iota((1, 8), 1)
    speed = jnp.zeros((1, 8), F32)
    for c in range(CLASSES):
        speed = jnp.where(lane // 2 == c, thermal_ref[c], speed)
    sign = jnp.where(lane % 2 == 0, 1.0, -1.0)
    added = (0.5 * wave_bound * courant) * speed * packed.T + (0.5 * courant) * (sign * speed) * moved
    lane = iota((modes, columns), 1)
    for c in range(CLASSES):
        part = pl.ds(c * modes, modes)
        first = jnp.broadcast_to(added[:, 2 * c : 2 * c + 1], (modes, columns))
        last = jnp.broadcast_to(added[:, 2 * c + 1 : 2 * c + 2], (modes, columns))
        base_ref[part] = base_ref[part] + jnp.where(lane == 0, first, jnp.where(lane == columns - 1, last, 0.0))


def ends(target, thermal, inner, high, low, ring, left, right, totals):
    terms, columns = totals[0].shape
    return pl.pallas_call(
        ends_kernel,
        in_specs=[SMEM, SMEM] + [VMEM] * (6 + len(totals)),
        out_shape=(
            pltpu.VMEM(inner.shape, F32),
            pltpu.VMEM((terms, len(totals) * columns), F32),
        ),
        out_specs=(VMEM, VMEM),
        input_output_aliases={2: 0},
        compiler_params=PARAMS,
        name="ends",
    )(target, thermal, inner, high, low, ring, left, right, *totals)


def place_kernel(target_ref, _, *refs):
    arrived, (collision_ref, base_ref, out_hbm, collision_hbm, sems) = refs[:-5], refs[-5:]
    terms = arrived[0].shape[0]
    me, group = lax.axis_index("mode"), lax.axis_size("mode")
    copies = [pltpu.make_async_copy(collision_ref, collision_hbm, sems.at[0])]
    for r, terms_ref in enumerate(arrived, 1):
        first = lax.rem(me + r, group) * terms
        values = collision_update * terms_ref[...].astype(F32)
        for j in range(terms):
            row = pl.ds(target_ref[first + j], 1)
            base_ref[row] = base_ref[row] + values[j : j + 1]
    copies.append(pltpu.make_async_copy(base_ref, out_hbm, sems.at[1]))
    copies[1].start()
    copies[0].start()
    for copy in copies:
        copy.wait()


def place(target, base, arrived, collision):
    return pl.pallas_call(
        place_kernel,
        in_specs=[SMEM, VMEM] + [VMEM] * (len(arrived) + 1),
        out_shape=(
            pltpu.VMEM(base.shape, F32),
            jax.ShapeDtypeStruct(base.shape, F32),
            jax.ShapeDtypeStruct(collision.shape, F32),
        ),
        out_specs=(VMEM, HBM, HBM),
        scratch_shapes=[pltpu.SemaphoreType.DMA((2,))],
        input_output_aliases={1: 0},
        compiler_params=PARAMS,
        name="place",
    )(target, base, *arrived, collision)


def shards(state, tensor, table, thermal, output_mode_row):
    rows = state.shape[0]
    terms, modes, _ = tensor.shape
    slabs, group = lax.axis_size("space"), lax.axis_size("mode")

    def shift(x, by):
        return lax.ppermute(x, "mode", [(i, (i + by) % group) for i in range(group)])

    columns = state.shape[1]
    flat = remain(jnp.transpose(tensor, (1, 0, 2)).reshape(modes * terms, rows))
    coarse, wide, index, speed, target, *held = coarsen(state, table.T, thermal, output_mode_row, flat)
    given = wide, index, speed, target, flat
    cells = [coarse] + [shift(coarse, r) for r in range(1, group)]

    lines = -(-rows // columns // 8) * 8
    edge, *held = preparing(early_kernel, *given, held, [coarse], extra=[pltpu.VMEM((lines, columns), BF16)])
    size = slabs * group
    pairs = [(s * group + group - 1, (s + 1) * group % size) for s in range(slabs)]
    ring = lax.ppermute(edge, ("space", "mode"), pairs + [(j, i) for i, j in pairs])
    held_tensor, high, low, inner, kind, own = preparing(late_kernel, *given, held)

    totals, sent = collide(held_tensor, kind, own, cells)
    arrived = [shift(x, group - r) for r, x in enumerate(sent, 1)]
    base, collision = ends(target, speed, inner, high, low, ring, cells[1], cells[group - 1], totals)
    return place(target, base, arrived, collision)[1:]


def solution(mesh):
    in_specs = (P(None, ("space", "mode")), P("mode", None, None), P(), P(), P())
    out_specs = (P(None, ("space", "mode")), P("mode", "space"))
    return jax.shard_map(shards, mesh=mesh, in_specs=in_specs, out_specs=out_specs, check_vma=False)
```

```python
import jax
import jax.numpy as jnp
from jax import lax
from jax.experimental import pallas as pl
from jax.experimental.pallas import tpu as pltpu
from jax.sharding import PartitionSpec as P

CLASSES = 3

wave_bound = 5.2
courant = 0.09
collision_update = 0.1

BF16 = jnp.bfloat16
F32 = jnp.float32
I32 = jnp.int32
VMEM = pl.BlockSpec(memory_space=pltpu.VMEM)
SMEM = pl.BlockSpec(memory_space=pltpu.SMEM)
HBM = pl.BlockSpec(memory_space=pltpu.HBM)
PARAMS = pltpu.CompilerParams(vmem_limit_bytes=16 * 2**20)


def remain(x):
    return pltpu.with_memory_space_constraint(x, pltpu.HBM)


def dot(a, b):
    return jnp.dot(a, b, preferred_element_type=F32)


def dot_general(a, b, da, db):
    return lax.dot_general(a, b, (((da,), (db,)), ((), ())), preferred_element_type=F32)


def halves(x):
    high = x.astype(BF16)
    return high, (x - high.astype(F32)).astype(BF16)


def iota(shape, axis):
    return lax.broadcasted_iota(I32, shape, axis)


def coarsen_kernel(state_hbm, *refs):
    small_hbm, tensor_hbm, coarse_ref, state_ref, small = refs[:3], refs[3], refs[4], refs[5], refs[6:9]
    outs, (sems, *scratch) = refs[9:15], refs[15:]
    rows = state_ref.shape[0]
    parts = [pl.ds(0, rows)]
    copies = [
        pltpu.make_async_copy(state_hbm.at[part], state_ref.at[part], sems.at[j])
        for j, part in enumerate(parts)
    ]
    copies += [
        pltpu.make_async_copy(source, target, sems.at[len(parts) + j])
        for j, (source, target) in enumerate(zip(small_hbm, small))
    ]
    for copy in copies:
        copy.start()
    for part, copy in zip(parts, copies):
        copy.wait()
        coarse_ref[part] = state_ref[part].astype(BF16)
    for copy in copies[len(parts) :]:
        copy.wait()

    @pl.when(stage() == FIRST)
    def _():
        prepare((state_ref, *small, tensor_hbm), outs, scratch, parts=2)


def coarsen(state, table, thermal, target, tensor):
    shapes = (
        pltpu.VMEM(state.shape, BF16),
        pltpu.VMEM(state.shape, F32),
        pltpu.VMEM(table.shape, I32),
        pltpu.SMEM(thermal.shape, F32),
        pltpu.SMEM(target.shape, I32),
    )
    held = held_shapes(tensor, state, table.shape[1])
    return pl.pallas_call(
        coarsen_kernel,
        in_specs=[HBM] * 5,
        out_shape=shapes + held,
        out_specs=(VMEM, VMEM, VMEM, SMEM, SMEM) + (VMEM,) * len(held),
        scratch_shapes=[
            pltpu.SemaphoreType.DMA((5,)),
            pltpu.VMEM(state.shape, F32),
            pltpu.SemaphoreType.DMA,
        ],
        compiler_params=PARAMS,
        name="coarsen",
    )(*(remain(x) for x in (state, table, thermal, target)), tensor)


def advection_halves(table_ref, high_ref, low_ref):
    modes = table_ref.shape[1]
    index = [table_ref[j : j + 1, :].astype(F32) for j in range(3)]
    row = iota((8, modes), 0)
    weighted = jnp.where(row == 0, 144.0 * index[0], jnp.where(row == 1, 12.0 * index[1], index[2]))
    weighted = jnp.where(row < 3, weighted, 0.0).astype(BF16)
    along = jnp.where(row == 0, index[0], 0.0).astype(BF16)
    ones = jnp.ones((8, modes), BF16)
    code_down = dot_general(weighted, ones, 0, 0)
    along_down = dot_general(along, ones, 0, 0)
    code_across = 144.0 * index[0] + 12.0 * index[1] + index[2]
    matrix = jnp.where(code_across == code_down - 144.0, jnp.sqrt(along_down), 0.0)
    matrix = matrix + jnp.where(code_across == code_down + 144.0, jnp.sqrt(along_down + 1.0), 0.0)
    high_ref[...], low_ref[...] = halves(matrix)


def inner_transport(state_ref, high_ref, low_ref, thermal_ref, out_ref, diff_ref):
    rows, columns = state_ref.shape
    modes = high_ref.shape[0]
    state = state_ref[...]
    lane = iota((rows, columns), 1)
    before = jnp.where(lane == 0, 0.0, pltpu.roll(state, 1, 1))
    after = jnp.where(lane == columns - 1, 0.0, pltpu.roll(state, columns - 1, 1))
    diff_ref[...] = after - before
    out_ref[...] = before + after - 2.0 * state
    for c in range(CLASSES):
        part = pl.ds(c * modes, modes)
        d_high, d_low = halves(diff_ref[part])
        moved = dot(high_ref[...], d_high) + dot(high_ref[...], d_low) + dot(low_ref[...], d_high)
        diffused = (0.5 * wave_bound * courant) * out_ref[part]
        out_ref[part] = state_ref[part] + thermal_ref[c] * (diffused - (0.5 * courant) * moved)


def prepare(given, outs, scratch, parts=1):
    state_ref, table_ref, thermal_ref, target_ref, tensor_hbm = given
    tensor_ref, high_ref, low_ref, inner_ref, kind_ref, own_ref = outs
    diff_ref, sem = scratch
    modes = high_ref.shape[0]
    rows = tensor_ref.shape[0]
    size = -(-rows // parts // 16) * 16
    pieces = [pl.ds(start, min(size, rows - start)) for start in range(0, rows, size)]
    copies = [pltpu.make_async_copy(tensor_hbm.at[piece], tensor_ref.at[piece], sem) for piece in pieces]
    kind_ref[...] = classes(target_ref, lax.axis_index("mode") * kind_ref.shape[0], kind_ref.shape, modes)
    own_ref[...] = state_ref[...].astype(BF16).astype(F32)
    copies[0].start()
    advection_halves(table_ref, high_ref, low_ref)
    inner_transport(state_ref, high_ref, low_ref, thermal_ref, inner_ref, diff_ref)
    copies[0].wait()
    for copy in copies[1:]:
        copy.start()
        copy.wait()


FIRST, EARLY, LATE = range(3)


def stage():
    slab = lax.axis_index("space")
    return jnp.where(slab == 1, FIRST, jnp.where(slab == 0, EARLY, LATE))


def early_kernel(state_ref, table_ref, thermal_ref, target_ref, tensor_hbm, coarse_ref, *refs):
    edge_ref, outs, scratch = refs[6], refs[7:13], refs[13:]
    given = state_ref, table_ref, thermal_ref, target_ref, tensor_hbm
    edge_row(coarse_ref, edge_ref)

    @pl.when(stage() == EARLY)
    def _():
        prepare(given, outs, scratch)


def edge_row(coarse_ref, edge_ref):
    rows, columns = coarse_ref.shape
    wanted = jnp.where(lax.axis_index("mode") == 0, 0, columns - 1)
    pick = (iota((8, columns), 1) == wanted).astype(BF16)
    edge = dot_general(pick, coarse_ref[...], 1, 1)
    lines = edge_ref.shape[0]
    edge = jnp.concatenate([edge, jnp.zeros((8, lines * columns - rows), F32)], axis=1)
    folded = [edge[0:1, j * columns : (j + 1) * columns] for j in range(lines)]
    edge_ref[...] = jnp.concatenate(folded).astype(BF16)


def late_kernel(state_ref, table_ref, thermal_ref, target_ref, tensor_hbm, *refs):
    @pl.when(stage() == LATE)
    def _():
        prepare((state_ref, table_ref, thermal_ref, target_ref, tensor_hbm), refs[6:12], refs[12:])


def held_shapes(tensor, state, modes):
    return (
        pltpu.VMEM(tensor.shape, BF16),
        pltpu.VMEM((modes, modes), BF16),
        pltpu.VMEM((modes, modes), BF16),
        pltpu.VMEM(state.shape, F32),
        pltpu.VMEM((tensor.shape[0] // modes, 2 * state.shape[1]), I32),
        pltpu.VMEM(state.shape, F32),
    )


def preparing(kernel, state, table, thermal, target, tensor, held, coarse=(), extra=()):
    shapes = tuple(extra) + held_shapes(tensor, state, table.shape[1])
    given = 5 + len(coarse)
    return pl.pallas_call(
        kernel,
        in_specs=[VMEM, VMEM, SMEM, SMEM, HBM] + [VMEM] * (len(coarse) + len(held)),
        out_shape=shapes,
        out_specs=(VMEM,) * len(shapes),
        scratch_shapes=[pltpu.VMEM(state.shape, F32), pltpu.SemaphoreType.DMA],
        input_output_aliases={given + j: len(extra) + j for j in range(len(held))},
        compiler_params=PARAMS,
        name=kernel.__name__,
    )(state, table, thermal, target, tensor, *coarse, *held)


def classes(target_ref, first, shape, modes):
    line = iota(shape, 0)
    kind = jnp.zeros(shape, I32)
    for j in range(shape[0]):
        target = target_ref[first + j]
        own_class = sum((target >= c * modes).astype(I32) for c in range(1, CLASSES))
        kind = jnp.where(line == j, own_class, kind)
    return kind


def contract(tensor_ref, cells, wide, kind):
    terms, columns = kind.shape
    modes = tensor_ref.shape[0] // terms
    product = dot(tensor_ref[...], cells).reshape(modes, terms, columns)
    sums = [jnp.zeros((terms, columns), F32) for _ in range(2)]

    def row(j):
        rows = [jnp.broadcast_to(ref[pl.ds(j, 1)], (terms, ref.shape[1])) for ref in wide]
        return jnp.concatenate(rows, axis=1)

    for i in range(modes):
        first = row(i)
        for c in range(1, CLASSES):
            first = jnp.where(kind == c, row(c * modes + i), first)
        sums[i % 2] = sums[i % 2] + first * product[i]
    return sums[0] + sums[1]


def collide_kernel(tensor_ref, kind_ref, own_ref, *refs):
    sets = len(refs) // 3
    given, totals, sent, wide_refs = refs[:sets], refs[sets : 2 * sets], refs[2 * sets : -1], refs[-1]
    columns = totals[0].shape[1]
    for at in range(0, sets, 2):
        pair = given[at : at + 2]
        cells = jnp.concatenate([ref[...] for ref in pair], axis=1)
        wide = []
        for j, ref in enumerate(pair):
            if at + j == 0:
                wide.append(own_ref)
            else:
                wide.append(wide_refs.at[j])
                wide_refs[j] = ref[...].astype(F32)
        total = contract(tensor_ref, cells, wide, kind_ref[:, 0 : len(pair) * columns])
        for j in range(len(pair)):
            part = total[:, j * columns : (j + 1) * columns]
            totals[at + j][...] = part
            if at + j > 0:
                sent[at + j - 1][...] = part.astype(BF16)


def collide(tensor, kind, own, cells):
    sets = len(cells)
    columns = cells[0].shape[1]
    terms = kind.shape[0]
    shapes = [pltpu.VMEM((terms, columns), F32)] * sets + [pltpu.VMEM((terms, columns), BF16)] * (sets - 1)
    found = pl.pallas_call(
        collide_kernel,
        in_specs=[VMEM] * (3 + sets),
        out_shape=tuple(shapes),
        out_specs=(VMEM,) * len(shapes),
        scratch_shapes=[pltpu.VMEM((2, *own.shape), F32)],
        compiler_params=PARAMS,
        name="collide",
    )(tensor, kind, own, *cells)
    return found[:sets], found[sets:]


def own_ends_kernel(target_ref, inner_ref, left_ref, right_ref, *refs):
    totals, base_ref, collision_ref, beyond_ref = refs[:-3], *refs[-3:]
    columns = inner_ref.shape[1]
    me, group = lax.axis_index("mode"), lax.axis_size("mode")
    terms = totals[0].shape[0]
    for r, terms_ref in enumerate(totals):
        start = pl.multiple_of(lax.rem(me + group - r, group) * columns, columns)
        collision_ref[:, pl.ds(start, columns)] = terms_ref[...]
    for j in range(terms):
        row = pl.ds(target_ref[me * terms + j], 1)
        base_ref[row] = base_ref[row] + collision_update * totals[0][j : j + 1]
    line, lane = iota((8, columns), 0), iota((8, columns), 1)
    last = jnp.logical_and(line == 0, lane == columns - 1)
    first = jnp.logical_and(line == 1, lane == 0)
    if group == 2:
        beyond = dot_general(jnp.logical_or(last, first).astype(BF16), left_ref[...], 1, 1)
    else:
        beyond = dot_general(last.astype(BF16), left_ref[...], 1, 1)
        beyond = beyond + dot_general(first.astype(BF16), right_ref[...], 1, 1)
    beyond_ref[...] = beyond


def own_ends(target, inner, left, right, totals):
    terms, columns = totals[0].shape
    return pl.pallas_call(
        own_ends_kernel,
        in_specs=[SMEM] + [VMEM] * (3 + len(totals)),
        out_shape=(
            pltpu.VMEM(inner.shape, F32),
            pltpu.VMEM((terms, len(totals) * columns), F32),
            pltpu.VMEM((8, inner.shape[0]), F32),
        ),
        out_specs=(VMEM,) * 3,
        input_output_aliases={1: 0},
        compiler_params=PARAMS,
        name="own_ends",
    )(target, inner, left, right, *totals)


def ends_kernel(thermal_ref, inner_ref, high_ref, low_ref, ring_ref, beyond_ref, base_ref):
    rows, columns = inner_ref.shape
    modes = high_ref.shape[0]
    me, group = lax.axis_index("mode"), lax.axis_size("mode")
    beyond = beyond_ref[...]
    ring = ring_ref[...].astype(F32)
    ring = jnp.concatenate([ring[j : j + 1] for j in range(-(-rows // columns))], axis=1)[:, 0:rows]
    ends_of = jnp.where(me == 0, ring, beyond[0:1]), jnp.where(me == group - 1, ring, beyond[1:2])
    line = iota((8, modes), 0)
    packed = jnp.zeros((8, modes), F32)
    for c in range(CLASSES):
        for side, end in enumerate(ends_of):
            packed = jnp.where(line == 2 * c + side, end[:, c * modes : (c + 1) * modes], packed)
    coarse = packed.astype(BF16)
    moved = dot_general(high_ref[...], coarse, 1, 1) + dot_general(low_ref[...], coarse, 1, 1)
    lane = iota((1, 8), 1)
    speed = jnp.zeros((1, 8), F32)
    for c in range(CLASSES):
        speed = jnp.where(lane // 2 == c, thermal_ref[c], speed)
    sign = jnp.where(lane % 2 == 0, 1.0, -1.0)
    added = (0.5 * wave_bound * courant) * speed * packed.T + (0.5 * courant) * (sign * speed) * moved
    lane = iota((modes, columns), 1)
    for c in range(CLASSES):
        part = pl.ds(c * modes, modes)
        first = jnp.broadcast_to(added[:, 2 * c : 2 * c + 1], (modes, columns))
        last = jnp.broadcast_to(added[:, 2 * c + 1 : 2 * c + 2], (modes, columns))
        base_ref[part] = base_ref[part] + jnp.where(lane == 0, first, jnp.where(lane == columns - 1, last, 0.0))


def ends(thermal, inner, high, low, ring, beyond):
    return pl.pallas_call(
        ends_kernel,
        in_specs=[SMEM] + [VMEM] * 5,
        out_shape=pltpu.VMEM(inner.shape, F32),
        out_specs=VMEM,
        input_output_aliases={1: 0},
        compiler_params=PARAMS,
        name="ends",
    )(thermal, inner, high, low, ring, beyond)


def place_kernel(target_ref, _, *refs):
    arrived, (collision_ref, base_ref, out_hbm, collision_hbm, sems) = refs[:-5], refs[-5:]
    terms = arrived[0].shape[0]
    me, group = lax.axis_index("mode"), lax.axis_size("mode")
    copies = [pltpu.make_async_copy(collision_ref, collision_hbm, sems.at[0])]
    for r, terms_ref in enumerate(arrived, 1):
        first = lax.rem(me + r, group) * terms
        values = collision_update * terms_ref[...].astype(F32)
        for j in range(terms):
            row = pl.ds(target_ref[first + j], 1)
            base_ref[row] = base_ref[row] + values[j : j + 1]
    copies.append(pltpu.make_async_copy(base_ref, out_hbm, sems.at[1]))
    copies[1].start()
    copies[0].start()
    for copy in copies:
        copy.wait()


def place(target, base, arrived, collision):
    return pl.pallas_call(
        place_kernel,
        in_specs=[SMEM, VMEM] + [VMEM] * (len(arrived) + 1),
        out_shape=(
            pltpu.VMEM(base.shape, F32),
            jax.ShapeDtypeStruct(base.shape, F32),
            jax.ShapeDtypeStruct(collision.shape, F32),
        ),
        out_specs=(VMEM, HBM, HBM),
        scratch_shapes=[pltpu.SemaphoreType.DMA((2,))],
        input_output_aliases={1: 0},
        compiler_params=PARAMS,
        name="place",
    )(target, base, *arrived, collision)


def shards(state, tensor, table, thermal, output_mode_row):
    rows = state.shape[0]
    terms, modes, _ = tensor.shape
    slabs, group = lax.axis_size("space"), lax.axis_size("mode")

    def shift(x, by):
        return lax.ppermute(x, "mode", [(i, (i + by) % group) for i in range(group)])

    columns = state.shape[1]
    flat = remain(jnp.transpose(tensor, (1, 0, 2)).reshape(modes * terms, rows))
    coarse, wide, index, speed, target, *held = coarsen(state, table.T, thermal, output_mode_row, flat)
    given = wide, index, speed, target, flat
    cells = [coarse] + [shift(coarse, r) for r in range(1, group)]

    lines = -(-rows // columns // 8) * 8
    edge, *held = preparing(early_kernel, *given, held, [coarse], extra=[pltpu.VMEM((lines, columns), BF16)])
    size = slabs * group
    pairs = [(s * group + group - 1, (s + 1) * group % size) for s in range(slabs)]
    ring = lax.ppermute(edge, ("space", "mode"), pairs + [(j, i) for i, j in pairs])
    held_tensor, high, low, inner, kind, own = preparing(late_kernel, *given, held)

    totals, sent = collide(held_tensor, kind, own, cells)
    arrived = [shift(x, group - r) for r, x in enumerate(sent, 1)]
    base, collision, beyond = own_ends(target, inner, cells[1], cells[group - 1], totals)
    base = ends(speed, base, high, low, ring, beyond)
    return place(target, base, arrived, collision)[1:]


def solution(mesh):
    in_specs = (P(None, ("space", "mode")), P("mode", None, None), P(), P(), P())
    out_specs = (P(None, ("space", "mode")), P("mode", "space"))
    return jax.shard_map(shards, mesh=mesh, in_specs=in_specs, out_specs=out_specs, check_vma=False)
```

```python
import jax
import jax.numpy as jnp
from jax import lax
from jax.experimental import pallas as pl
from jax.experimental.pallas import tpu as pltpu
from jax.sharding import PartitionSpec as P

CLASSES = 3

wave_bound = 5.2
courant = 0.09
collision_update = 0.1

BF16 = jnp.bfloat16
F32 = jnp.float32
I32 = jnp.int32
VMEM = pl.BlockSpec(memory_space=pltpu.VMEM)
SMEM = pl.BlockSpec(memory_space=pltpu.SMEM)
HBM = pl.BlockSpec(memory_space=pltpu.HBM)
PARAMS = pltpu.CompilerParams(vmem_limit_bytes=16 * 2**20)


def remain(x):
    return pltpu.with_memory_space_constraint(x, pltpu.HBM)


def dot(a, b):
    return jnp.dot(a, b, preferred_element_type=F32)


def dot_general(a, b, da, db):
    return lax.dot_general(a, b, (((da,), (db,)), ((), ())), preferred_element_type=F32)


def halves(x):
    high = x.astype(BF16)
    return high, (x - high.astype(F32)).astype(BF16)


def iota(shape, axis):
    return lax.broadcasted_iota(I32, shape, axis)


def coarsen_kernel(state_hbm, *refs):
    small_hbm, tensor_hbm, coarse_ref, state_ref, small = refs[:3], refs[3], refs[4], refs[5], refs[6:9]
    outs, (sems, *scratch) = refs[9:15], refs[15:]
    rows = state_ref.shape[0]
    parts = [pl.ds(0, rows)]
    copies = [
        pltpu.make_async_copy(state_hbm.at[part], state_ref.at[part], sems.at[j])
        for j, part in enumerate(parts)
    ]
    copies += [
        pltpu.make_async_copy(source, target, sems.at[len(parts) + j])
        for j, (source, target) in enumerate(zip(small_hbm, small))
    ]
    for copy in copies:
        copy.start()
    for part, copy in zip(parts, copies):
        copy.wait()
        coarse_ref[part] = state_ref[part].astype(BF16)
    for copy in copies[len(parts) :]:
        copy.wait()

    @pl.when(stage() == FIRST)
    def _():
        prepare((state_ref, *small, tensor_hbm), outs, scratch, parts=2)


def coarsen(state, table, thermal, target, tensor):
    shapes = (
        pltpu.VMEM(state.shape, BF16),
        pltpu.VMEM(state.shape, F32),
        pltpu.VMEM(table.shape, I32),
        pltpu.SMEM(thermal.shape, F32),
        pltpu.SMEM(target.shape, I32),
    )
    held = held_shapes(tensor, state, table.shape[1])
    return pl.pallas_call(
        coarsen_kernel,
        in_specs=[HBM] * 5,
        out_shape=shapes + held,
        out_specs=(VMEM, VMEM, VMEM, SMEM, SMEM) + (VMEM,) * len(held),
        scratch_shapes=[
            pltpu.SemaphoreType.DMA((5,)),
            pltpu.VMEM(state.shape, F32),
            pltpu.SemaphoreType.DMA,
        ],
        compiler_params=PARAMS,
        name="coarsen",
    )(*(remain(x) for x in (state, table, thermal, target)), tensor)


def advection_halves(table_ref, high_ref, low_ref):
    modes = table_ref.shape[1]
    index = [table_ref[j : j + 1, :].astype(F32) for j in range(3)]
    row = iota((8, modes), 0)
    weighted = jnp.where(row == 0, 144.0 * index[0], jnp.where(row == 1, 12.0 * index[1], index[2]))
    weighted = jnp.where(row < 3, weighted, 0.0).astype(BF16)
    along = jnp.where(row == 0, index[0], 0.0).astype(BF16)
    ones = jnp.ones((8, modes), BF16)
    code_down = dot_general(weighted, ones, 0, 0)
    along_down = dot_general(along, ones, 0, 0)
    code_across = 144.0 * index[0] + 12.0 * index[1] + index[2]
    matrix = jnp.where(code_across == code_down - 144.0, jnp.sqrt(along_down), 0.0)
    matrix = matrix + jnp.where(code_across == code_down + 144.0, jnp.sqrt(along_down + 1.0), 0.0)
    high_ref[...], low_ref[...] = halves(matrix)


def inner_transport(state_ref, high_ref, low_ref, thermal_ref, out_ref, diff_ref):
    rows, columns = state_ref.shape
    modes = high_ref.shape[0]
    state = state_ref[...]
    lane = iota((rows, columns), 1)
    before = jnp.where(lane == 0, 0.0, pltpu.roll(state, 1, 1))
    after = jnp.where(lane == columns - 1, 0.0, pltpu.roll(state, columns - 1, 1))
    diff_ref[...] = after - before
    out_ref[...] = before + after - 2.0 * state
    for c in range(CLASSES):
        part = pl.ds(c * modes, modes)
        d_high, d_low = halves(diff_ref[part])
        moved = dot(high_ref[...], d_high) + dot(high_ref[...], d_low) + dot(low_ref[...], d_high)
        diffused = (0.5 * wave_bound * courant) * out_ref[part]
        out_ref[part] = state_ref[part] + thermal_ref[c] * (diffused - (0.5 * courant) * moved)


def prepare(given, outs, scratch, parts=1):
    state_ref, table_ref, thermal_ref, target_ref, tensor_hbm = given
    tensor_ref, high_ref, low_ref, inner_ref, kind_ref, own_ref = outs
    diff_ref, sem = scratch
    modes = high_ref.shape[0]
    rows = tensor_ref.shape[0]
    size = -(-rows // parts // 16) * 16
    pieces = [pl.ds(start, min(size, rows - start)) for start in range(0, rows, size)]
    copies = [pltpu.make_async_copy(tensor_hbm.at[piece], tensor_ref.at[piece], sem) for piece in pieces]
    kind_ref[...] = classes(target_ref, lax.axis_index("mode") * kind_ref.shape[0], kind_ref.shape, modes)
    own_ref[...] = state_ref[...].astype(BF16).astype(F32)
    copies[0].start()
    advection_halves(table_ref, high_ref, low_ref)
    inner_transport(state_ref, high_ref, low_ref, thermal_ref, inner_ref, diff_ref)
    copies[0].wait()
    for copy in copies[1:]:
        copy.start()
        copy.wait()


FIRST, EARLY, LATE = range(3)


def stage():
    slab = lax.axis_index("space")
    return jnp.where(slab == 1, FIRST, jnp.where(slab == 0, EARLY, LATE))


def early_kernel(state_ref, table_ref, thermal_ref, target_ref, tensor_hbm, coarse_ref, *refs):
    edge_ref, outs, scratch = refs[6], refs[7:13], refs[13:]
    given = state_ref, table_ref, thermal_ref, target_ref, tensor_hbm
    edge_row(coarse_ref, edge_ref)

    @pl.when(stage() == EARLY)
    def _():
        prepare(given, outs, scratch)


def edge_row(coarse_ref, edge_ref):
    rows, columns = coarse_ref.shape
    wanted = jnp.where(lax.axis_index("mode") == 0, 0, columns - 1)
    pick = (iota((8, columns), 1) == wanted).astype(BF16)
    edge = dot_general(pick, coarse_ref[...], 1, 1)
    lines = edge_ref.shape[0]
    edge = jnp.concatenate([edge, jnp.zeros((8, lines * columns - rows), F32)], axis=1)
    folded = [edge[0:1, j * columns : (j + 1) * columns] for j in range(lines)]
    edge_ref[...] = jnp.concatenate(folded).astype(BF16)


def late_kernel(state_ref, table_ref, thermal_ref, target_ref, tensor_hbm, *refs):
    @pl.when(stage() == LATE)
    def _():
        prepare((state_ref, table_ref, thermal_ref, target_ref, tensor_hbm), refs[6:12], refs[12:])


def held_shapes(tensor, state, modes):
    return (
        pltpu.VMEM(tensor.shape, BF16),
        pltpu.VMEM((modes, modes), BF16),
        pltpu.VMEM((modes, modes), BF16),
        pltpu.VMEM(state.shape, F32),
        pltpu.VMEM((tensor.shape[0] // modes, 2 * state.shape[1]), I32),
        pltpu.VMEM(state.shape, F32),
    )


def preparing(kernel, state, table, thermal, target, tensor, held, coarse=(), extra=()):
    shapes = tuple(extra) + held_shapes(tensor, state, table.shape[1])
    given = 5 + len(coarse)
    return pl.pallas_call(
        kernel,
        in_specs=[VMEM, VMEM, SMEM, SMEM, HBM] + [VMEM] * (len(coarse) + len(held)),
        out_shape=shapes,
        out_specs=(VMEM,) * len(shapes),
        scratch_shapes=[pltpu.VMEM(state.shape, F32), pltpu.SemaphoreType.DMA],
        input_output_aliases={given + j: len(extra) + j for j in range(len(held))},
        compiler_params=PARAMS,
        name=kernel.__name__,
    )(state, table, thermal, target, tensor, *coarse, *held)


def classes(target_ref, first, shape, modes):
    line = iota(shape, 0)
    kind = jnp.zeros(shape, I32)
    for j in range(shape[0]):
        target = target_ref[first + j]
        own_class = sum((target >= c * modes).astype(I32) for c in range(1, CLASSES))
        kind = jnp.where(line == j, own_class, kind)
    return kind


def contract(tensor_ref, cells, wide, kind):
    terms, columns = kind.shape
    modes = tensor_ref.shape[0] // terms
    product = dot(tensor_ref[...], cells).reshape(modes, terms, columns)
    sums = [jnp.zeros((terms, columns), F32) for _ in range(2)]

    def row(j):
        rows = [jnp.broadcast_to(ref[pl.ds(j, 1)], (terms, ref.shape[1])) for ref in wide]
        return jnp.concatenate(rows, axis=1)

    for i in range(modes):
        first = row(i)
        for c in range(1, CLASSES):
            first = jnp.where(kind == c, row(c * modes + i), first)
        sums[i % 2] = sums[i % 2] + first * product[i]
    return sums[0] + sums[1]


def collide_kernel(tensor_ref, kind_ref, own_ref, *refs):
    sets = len(refs) // 3
    given, totals, sent, wide_refs = refs[:sets], refs[sets : 2 * sets], refs[2 * sets : -1], refs[-1]
    columns = totals[0].shape[1]
    for at in range(0, sets, 2):
        pair = given[at : at + 2]
        cells = jnp.concatenate([ref[...] for ref in pair], axis=1)
        wide = []
        for j, ref in enumerate(pair):
            if at + j == 0:
                wide.append(own_ref)
            else:
                wide.append(wide_refs.at[j])
                wide_refs[j] = ref[...].astype(F32)
        total = contract(tensor_ref, cells, wide, kind_ref[:, 0 : len(pair) * columns])
        for j in range(len(pair)):
            part = total[:, j * columns : (j + 1) * columns]
            totals[at + j][...] = part
            if at + j > 0:
                sent[at + j - 1][...] = part.astype(BF16)


def collide(tensor, kind, own, cells):
    sets = len(cells)
    columns = cells[0].shape[1]
    terms = kind.shape[0]
    shapes = [pltpu.VMEM((terms, columns), F32)] * sets + [pltpu.VMEM((terms, columns), BF16)] * (sets - 1)
    found = pl.pallas_call(
        collide_kernel,
        in_specs=[VMEM] * (3 + sets),
        out_shape=tuple(shapes),
        out_specs=(VMEM,) * len(shapes),
        scratch_shapes=[pltpu.VMEM((2, *own.shape), F32)],
        compiler_params=PARAMS,
        name="collide",
    )(tensor, kind, own, *cells)
    return found[:sets], found[sets:]


def own_ends_kernel(target_ref, inner_ref, left_ref, right_ref, *refs):
    totals, base_ref, collision_ref, beyond_ref = refs[:-3], *refs[-3:]
    columns = inner_ref.shape[1]
    me, group = lax.axis_index("mode"), lax.axis_size("mode")
    terms = totals[0].shape[0]
    for r, terms_ref in enumerate(totals):
        start = pl.multiple_of(lax.rem(me + group - r, group) * columns, columns)
        collision_ref[:, pl.ds(start, columns)] = terms_ref[...]
    for j in range(terms):
        row = pl.ds(target_ref[me * terms + j], 1)
        base_ref[row] = base_ref[row] + collision_update * totals[0][j : j + 1]
    line, lane = iota((8, columns), 0), iota((8, columns), 1)
    last = jnp.logical_and(line == 0, lane == columns - 1)
    first = jnp.logical_and(line == 1, lane == 0)
    if group == 2:
        beyond = dot_general(jnp.logical_or(last, first).astype(BF16), left_ref[...], 1, 1)
    else:
        beyond = dot_general(last.astype(BF16), left_ref[...], 1, 1)
        beyond = beyond + dot_general(first.astype(BF16), right_ref[...], 1, 1)
    beyond_ref[...] = beyond


def own_ends(target, inner, left, right, totals):
    terms, columns = totals[0].shape
    return pl.pallas_call(
        own_ends_kernel,
        in_specs=[SMEM] + [VMEM] * (3 + len(totals)),
        out_shape=(
            pltpu.VMEM(inner.shape, F32),
            pltpu.VMEM((terms, len(totals) * columns), F32),
            pltpu.VMEM((8, inner.shape[0]), F32),
        ),
        out_specs=(VMEM,) * 3,
        input_output_aliases={1: 0},
        compiler_params=PARAMS,
        name="own_ends",
    )(target, inner, left, right, *totals)


def ends_kernel(thermal_ref, inner_ref, high_ref, low_ref, ring_ref, beyond_ref, base_ref):
    rows, columns = inner_ref.shape
    modes = high_ref.shape[0]
    me, group = lax.axis_index("mode"), lax.axis_size("mode")
    beyond = beyond_ref[...]
    ring = ring_ref[...].astype(F32)
    ring = jnp.concatenate([ring[j : j + 1] for j in range(-(-rows // columns))], axis=1)[:, 0:rows]
    ends_of = jnp.where(me == 0, ring, beyond[0:1]), jnp.where(me == group - 1, ring, beyond[1:2])
    line = iota((8, modes), 0)
    packed = jnp.zeros((8, modes), F32)
    for c in range(CLASSES):
        for side, end in enumerate(ends_of):
            packed = jnp.where(line == 2 * c + side, end[:, c * modes : (c + 1) * modes], packed)
    coarse = packed.astype(BF16)
    moved = dot_general(high_ref[...], coarse, 1, 1) + dot_general(low_ref[...], coarse, 1, 1)
    lane = iota((1, 8), 1)
    speed = jnp.zeros((1, 8), F32)
    for c in range(CLASSES):
        speed = jnp.where(lane // 2 == c, thermal_ref[c], speed)
    sign = jnp.where(lane % 2 == 0, 1.0, -1.0)
    added = (0.5 * wave_bound * courant) * speed * packed.T + (0.5 * courant) * (sign * speed) * moved
    added = jnp.concatenate(halves(added), axis=1)
    line, lane = iota((16, columns), 0) % 8, iota((16, columns), 1)
    for c in range(CLASSES):
        part = pl.ds(c * modes, modes)
        first = jnp.logical_and(line == 2 * c, lane == 0)
        last = jnp.logical_and(line == 2 * c + 1, lane == columns - 1)
        base_ref[part] = base_ref[part] + dot(added, jnp.logical_or(first, last).astype(BF16))


def ends(thermal, inner, high, low, ring, beyond):
    return pl.pallas_call(
        ends_kernel,
        in_specs=[SMEM] + [VMEM] * 5,
        out_shape=pltpu.VMEM(inner.shape, F32),
        out_specs=VMEM,
        input_output_aliases={1: 0},
        compiler_params=PARAMS,
        name="ends",
    )(thermal, inner, high, low, ring, beyond)


def place_kernel(target_ref, _, *refs):
    arrived, (collision_ref, base_ref, out_hbm, collision_hbm, sems) = refs[:-5], refs[-5:]
    terms = arrived[0].shape[0]
    me, group = lax.axis_index("mode"), lax.axis_size("mode")
    copies = [pltpu.make_async_copy(collision_ref, collision_hbm, sems.at[0])]
    for r, terms_ref in enumerate(arrived, 1):
        first = lax.rem(me + r, group) * terms
        values = collision_update * terms_ref[...].astype(F32)
        for j in range(terms):
            row = pl.ds(target_ref[first + j], 1)
            base_ref[row] = base_ref[row] + values[j : j + 1]
    copies.append(pltpu.make_async_copy(base_ref, out_hbm, sems.at[1]))
    copies[1].start()
    copies[0].start()
    for copy in copies:
        copy.wait()


def place(target, base, arrived, collision):
    return pl.pallas_call(
        place_kernel,
        in_specs=[SMEM, VMEM] + [VMEM] * (len(arrived) + 1),
        out_shape=(
            pltpu.VMEM(base.shape, F32),
            jax.ShapeDtypeStruct(base.shape, F32),
            jax.ShapeDtypeStruct(collision.shape, F32),
        ),
        out_specs=(VMEM, HBM, HBM),
        scratch_shapes=[pltpu.SemaphoreType.DMA((2,))],
        input_output_aliases={1: 0},
        compiler_params=PARAMS,
        name="place",
    )(target, base, *arrived, collision)


def shards(state, tensor, table, thermal, output_mode_row):
    rows = state.shape[0]
    terms, modes, _ = tensor.shape
    slabs, group = lax.axis_size("space"), lax.axis_size("mode")

    def shift(x, by):
        return lax.ppermute(x, "mode", [(i, (i + by) % group) for i in range(group)])

    columns = state.shape[1]
    flat = remain(jnp.transpose(tensor, (1, 0, 2)).reshape(modes * terms, rows))
    coarse, wide, index, speed, target, *held = coarsen(state, table.T, thermal, output_mode_row, flat)
    given = wide, index, speed, target, flat
    cells = [coarse] + [shift(coarse, r) for r in range(1, group)]

    lines = -(-rows // columns // 8) * 8
    edge, *held = preparing(early_kernel, *given, held, [coarse], extra=[pltpu.VMEM((lines, columns), BF16)])
    size = slabs * group
    pairs = [(s * group + group - 1, (s + 1) * group % size) for s in range(slabs)]
    ring = lax.ppermute(edge, ("space", "mode"), pairs + [(j, i) for i, j in pairs])
    held_tensor, high, low, inner, kind, own = preparing(late_kernel, *given, held)

    totals, sent = collide(held_tensor, kind, own, cells)
    arrived = [shift(x, group - r) for r, x in enumerate(sent, 1)]
    base, collision, beyond = own_ends(target, inner, cells[1], cells[group - 1], totals)
    base = ends(speed, base, high, low, ring, beyond)
    return place(target, base, arrived, collision)[1:]


def solution(mesh):
    in_specs = (P(None, ("space", "mode")), P("mode", None, None), P(), P(), P())
    out_specs = (P(None, ("space", "mode")), P("mode", "space"))
    return jax.shard_map(shards, mesh=mesh, in_specs=in_specs, out_specs=out_specs, check_vma=False)
```

```python
import jax
import jax.numpy as jnp
from jax import lax
from jax.experimental import pallas as pl
from jax.experimental.pallas import tpu as pltpu
from jax.sharding import PartitionSpec as P

CLASSES = 3

wave_bound = 5.2
courant = 0.09
collision_update = 0.1

BF16 = jnp.bfloat16
F32 = jnp.float32
I32 = jnp.int32
VMEM = pl.BlockSpec(memory_space=pltpu.VMEM)
SMEM = pl.BlockSpec(memory_space=pltpu.SMEM)
HBM = pl.BlockSpec(memory_space=pltpu.HBM)
PARAMS = pltpu.CompilerParams(vmem_limit_bytes=16 * 2**20)


def remain(x):
    return pltpu.with_memory_space_constraint(x, pltpu.HBM)


def dot(a, b):
    return jnp.dot(a, b, preferred_element_type=F32)


def dot_general(a, b, da, db):
    return lax.dot_general(a, b, (((da,), (db,)), ((), ())), preferred_element_type=F32)


def halves(x):
    high = x.astype(BF16)
    return high, (x - high.astype(F32)).astype(BF16)


def iota(shape, axis):
    return lax.broadcasted_iota(I32, shape, axis)


def coarsen_kernel(state_hbm, *refs):
    small_hbm, tensor_hbm, coarse_ref, state_ref, small = refs[:3], refs[3], refs[4], refs[5], refs[6:9]
    outs, (sems, *scratch) = refs[9:15], refs[15:]
    rows = state_ref.shape[0]
    parts = [pl.ds(0, rows)]
    copies = [
        pltpu.make_async_copy(state_hbm.at[part], state_ref.at[part], sems.at[j])
        for j, part in enumerate(parts)
    ]
    copies += [
        pltpu.make_async_copy(source, target, sems.at[len(parts) + j])
        for j, (source, target) in enumerate(zip(small_hbm, small))
    ]
    for copy in copies:
        copy.start()
    for part, copy in zip(parts, copies):
        copy.wait()
        coarse_ref[part] = state_ref[part].astype(BF16)
    for copy in copies[len(parts) :]:
        copy.wait()

    @pl.when(stage() == FIRST)
    def _():
        prepare((state_ref, *small, tensor_hbm), outs, scratch, parts=2)


def coarsen(state, table, thermal, target, tensor):
    shapes = (
        pltpu.VMEM(state.shape, BF16),
        pltpu.VMEM(state.shape, F32),
        pltpu.VMEM(table.shape, I32),
        pltpu.SMEM(thermal.shape, F32),
        pltpu.SMEM(target.shape, I32),
    )
    held = held_shapes(tensor, state, table.shape[1])
    return pl.pallas_call(
        coarsen_kernel,
        in_specs=[HBM] * 5,
        out_shape=shapes + held,
        out_specs=(VMEM, VMEM, VMEM, SMEM, SMEM) + (VMEM,) * len(held),
        scratch_shapes=[
            pltpu.SemaphoreType.DMA((5,)),
            pltpu.VMEM(state.shape, F32),
            pltpu.SemaphoreType.DMA,
        ],
        compiler_params=PARAMS,
        name="coarsen",
    )(*(remain(x) for x in (state, table, thermal, target)), tensor)


def advection_halves(table_ref, high_ref, low_ref):
    modes = table_ref.shape[1]
    index = [table_ref[j : j + 1, :].astype(F32) for j in range(3)]
    row = iota((8, modes), 0)
    weighted = jnp.where(row == 0, 144.0 * index[0], jnp.where(row == 1, 12.0 * index[1], index[2]))
    weighted = jnp.where(row < 3, weighted, 0.0).astype(BF16)
    along = jnp.where(row == 0, index[0], 0.0).astype(BF16)
    ones = jnp.ones((8, modes), BF16)
    code_down = dot_general(weighted, ones, 0, 0)
    along_down = dot_general(along, ones, 0, 0)
    code_across = 144.0 * index[0] + 12.0 * index[1] + index[2]
    matrix = jnp.where(code_across == code_down - 144.0, jnp.sqrt(along_down), 0.0)
    matrix = matrix + jnp.where(code_across == code_down + 144.0, jnp.sqrt(along_down + 1.0), 0.0)
    high_ref[...], low_ref[...] = halves(matrix)


def inner_transport(state_ref, high_ref, low_ref, thermal_ref, out_ref, diff_ref):
    rows, columns = state_ref.shape
    modes = high_ref.shape[0]
    state = state_ref[...]
    lane = iota((rows, columns), 1)
    before = jnp.where(lane == 0, 0.0, pltpu.roll(state, 1, 1))
    after = jnp.where(lane == columns - 1, 0.0, pltpu.roll(state, columns - 1, 1))
    diff_ref[...] = after - before
    out_ref[...] = before + after - 2.0 * state
    for c in range(CLASSES):
        part = pl.ds(c * modes, modes)
        d_high, d_low = halves(diff_ref[part])
        moved = dot(high_ref[...], d_high) + dot(high_ref[...], d_low) + dot(low_ref[...], d_high)
        diffused = (0.5 * wave_bound * courant) * out_ref[part]
        out_ref[part] = state_ref[part] + thermal_ref[c] * (diffused - (0.5 * courant) * moved)


def prepare(given, outs, scratch, parts=1):
    state_ref, table_ref, thermal_ref, target_ref, tensor_hbm = given
    tensor_ref, high_ref, low_ref, inner_ref, kind_ref, own_ref = outs
    diff_ref, sem = scratch
    modes = high_ref.shape[0]
    rows = tensor_ref.shape[0]
    size = -(-rows // parts // 16) * 16
    pieces = [pl.ds(start, min(size, rows - start)) for start in range(0, rows, size)]
    copies = [pltpu.make_async_copy(tensor_hbm.at[piece], tensor_ref.at[piece], sem) for piece in pieces]
    kind_ref[...] = classes(target_ref, lax.axis_index("mode") * kind_ref.shape[0], kind_ref.shape, modes)
    own_ref[...] = state_ref[...].astype(BF16).astype(F32)
    copies[0].start()
    advection_halves(table_ref, high_ref, low_ref)
    inner_transport(state_ref, high_ref, low_ref, thermal_ref, inner_ref, diff_ref)
    copies[0].wait()
    for copy in copies[1:]:
        copy.start()
        copy.wait()


FIRST, EARLY, LATE = range(3)


def stage():
    slab = lax.axis_index("space")
    first = jnp.logical_and(slab == 1, lax.axis_index("mode") > 0)
    return jnp.where(first, FIRST, jnp.where(slab <= 1, EARLY, LATE))


def early_kernel(state_ref, table_ref, thermal_ref, target_ref, tensor_hbm, coarse_ref, *refs):
    edge_ref, outs, scratch = refs[6], refs[7:13], refs[13:]
    given = state_ref, table_ref, thermal_ref, target_ref, tensor_hbm
    edge_row(coarse_ref, edge_ref)

    @pl.when(stage() == EARLY)
    def _():
        prepare(given, outs, scratch)


def edge_row(coarse_ref, edge_ref):
    rows, columns = coarse_ref.shape
    wanted = jnp.where(lax.axis_index("mode") == 0, 0, columns - 1)
    pick = (iota((8, columns), 1) == wanted).astype(BF16)
    edge = dot_general(pick, coarse_ref[...], 1, 1)
    lines = edge_ref.shape[0]
    edge = jnp.concatenate([edge, jnp.zeros((8, lines * columns - rows), F32)], axis=1)
    folded = [edge[0:1, j * columns : (j + 1) * columns] for j in range(lines)]
    edge_ref[...] = jnp.concatenate(folded).astype(BF16)


def late_kernel(state_ref, table_ref, thermal_ref, target_ref, tensor_hbm, *refs):
    @pl.when(stage() == LATE)
    def _():
        prepare((state_ref, table_ref, thermal_ref, target_ref, tensor_hbm), refs[6:12], refs[12:])


def held_shapes(tensor, state, modes):
    return (
        pltpu.VMEM(tensor.shape, BF16),
        pltpu.VMEM((modes, modes), BF16),
        pltpu.VMEM((modes, modes), BF16),
        pltpu.VMEM(state.shape, F32),
        pltpu.VMEM((tensor.shape[0] // modes, 2 * state.shape[1]), I32),
        pltpu.VMEM(state.shape, F32),
    )


def preparing(kernel, state, table, thermal, target, tensor, held, coarse=(), extra=()):
    shapes = tuple(extra) + held_shapes(tensor, state, table.shape[1])
    given = 5 + len(coarse)
    return pl.pallas_call(
        kernel,
        in_specs=[VMEM, VMEM, SMEM, SMEM, HBM] + [VMEM] * (len(coarse) + len(held)),
        out_shape=shapes,
        out_specs=(VMEM,) * len(shapes),
        scratch_shapes=[pltpu.VMEM(state.shape, F32), pltpu.SemaphoreType.DMA],
        input_output_aliases={given + j: len(extra) + j for j in range(len(held))},
        compiler_params=PARAMS,
        name=kernel.__name__,
    )(state, table, thermal, target, tensor, *coarse, *held)


def classes(target_ref, first, shape, modes):
    line = iota(shape, 0)
    kind = jnp.zeros(shape, I32)
    for j in range(shape[0]):
        target = target_ref[first + j]
        own_class = sum((target >= c * modes).astype(I32) for c in range(1, CLASSES))
        kind = jnp.where(line == j, own_class, kind)
    return kind


def contract(tensor_ref, cells, wide, kind):
    terms, columns = kind.shape
    modes = tensor_ref.shape[0] // terms
    product = dot(tensor_ref[...], cells).reshape(modes, terms, columns)
    sums = [jnp.zeros((terms, columns), F32) for _ in range(2)]

    def row(j):
        rows = [jnp.broadcast_to(ref[pl.ds(j, 1)], (terms, ref.shape[1])) for ref in wide]
        return jnp.concatenate(rows, axis=1)

    for i in range(modes):
        first = row(i)
        for c in range(1, CLASSES):
            first = jnp.where(kind == c, row(c * modes + i), first)
        sums[i % 2] = sums[i % 2] + first * product[i]
    return sums[0] + sums[1]


def collide_kernel(tensor_ref, kind_ref, own_ref, *refs):
    sets = len(refs) // 3
    given, totals, sent, wide_refs = refs[:sets], refs[sets : 2 * sets], refs[2 * sets : -1], refs[-1]
    columns = totals[0].shape[1]
    for at in range(0, sets, 2):
        pair = given[at : at + 2]
        cells = jnp.concatenate([ref[...] for ref in pair], axis=1)
        wide = []
        for j, ref in enumerate(pair):
            if at + j == 0:
                wide.append(own_ref)
            else:
                wide.append(wide_refs.at[j])
                wide_refs[j] = ref[...].astype(F32)
        total = contract(tensor_ref, cells, wide, kind_ref[:, 0 : len(pair) * columns])
        for j in range(len(pair)):
            part = total[:, j * columns : (j + 1) * columns]
            totals[at + j][...] = part
            if at + j > 0:
                sent[at + j - 1][...] = part.astype(BF16)


def collide(tensor, kind, own, cells):
    sets = len(cells)
    columns = cells[0].shape[1]
    terms = kind.shape[0]
    shapes = [pltpu.VMEM((terms, columns), F32)] * sets + [pltpu.VMEM((terms, columns), BF16)] * (sets - 1)
    found = pl.pallas_call(
        collide_kernel,
        in_specs=[VMEM] * (3 + sets),
        out_shape=tuple(shapes),
        out_specs=(VMEM,) * len(shapes),
        scratch_shapes=[pltpu.VMEM((2, *own.shape), F32)],
        compiler_params=PARAMS,
        name="collide",
    )(tensor, kind, own, *cells)
    return found[:sets], found[sets:]


def own_ends_kernel(target_ref, inner_ref, left_ref, right_ref, *refs):
    totals, base_ref, collision_ref, beyond_ref = refs[:-3], *refs[-3:]
    columns = inner_ref.shape[1]
    me, group = lax.axis_index("mode"), lax.axis_size("mode")
    terms = totals[0].shape[0]
    for r, terms_ref in enumerate(totals):
        start = pl.multiple_of(lax.rem(me + group - r, group) * columns, columns)
        collision_ref[:, pl.ds(start, columns)] = terms_ref[...]
    for j in range(terms):
        row = pl.ds(target_ref[me * terms + j], 1)
        base_ref[row] = base_ref[row] + collision_update * totals[0][j : j + 1]
    line, lane = iota((8, columns), 0), iota((8, columns), 1)
    last = jnp.logical_and(line == 0, lane == columns - 1)
    first = jnp.logical_and(line == 1, lane == 0)
    if group == 2:
        beyond = dot_general(jnp.logical_or(last, first).astype(BF16), left_ref[...], 1, 1)
    else:
        beyond = dot_general(last.astype(BF16), left_ref[...], 1, 1)
        beyond = beyond + dot_general(first.astype(BF16), right_ref[...], 1, 1)
    beyond_ref[...] = beyond


def own_ends(target, inner, left, right, totals):
    terms, columns = totals[0].shape
    return pl.pallas_call(
        own_ends_kernel,
        in_specs=[SMEM] + [VMEM] * (3 + len(totals)),
        out_shape=(
            pltpu.VMEM(inner.shape, F32),
            pltpu.VMEM((terms, len(totals) * columns), F32),
            pltpu.VMEM((8, inner.shape[0]), F32),
        ),
        out_specs=(VMEM,) * 3,
        input_output_aliases={1: 0},
        compiler_params=PARAMS,
        name="own_ends",
    )(target, inner, left, right, *totals)


def ends_kernel(thermal_ref, inner_ref, high_ref, low_ref, ring_ref, beyond_ref, base_ref):
    rows, columns = inner_ref.shape
    modes = high_ref.shape[0]
    me, group = lax.axis_index("mode"), lax.axis_size("mode")
    beyond = beyond_ref[...]
    ring = ring_ref[...].astype(F32)
    ring = jnp.concatenate([ring[j : j + 1] for j in range(-(-rows // columns))], axis=1)[:, 0:rows]
    ends_of = jnp.where(me == 0, ring, beyond[0:1]), jnp.where(me == group - 1, ring, beyond[1:2])
    line = iota((8, modes), 0)
    packed = jnp.zeros((8, modes), F32)
    for c in range(CLASSES):
        for side, end in enumerate(ends_of):
            packed = jnp.where(line == 2 * c + side, end[:, c * modes : (c + 1) * modes], packed)
    coarse = packed.astype(BF16)
    moved = dot_general(high_ref[...], coarse, 1, 1) + dot_general(low_ref[...], coarse, 1, 1)
    lane = iota((1, 8), 1)
    speed = jnp.zeros((1, 8), F32)
    for c in range(CLASSES):
        speed = jnp.where(lane // 2 == c, thermal_ref[c], speed)
    sign = jnp.where(lane % 2 == 0, 1.0, -1.0)
    added = (0.5 * wave_bound * courant) * speed * packed.T + (0.5 * courant) * (sign * speed) * moved
    added = jnp.concatenate(halves(added), axis=1)
    line, lane = iota((16, columns), 0) % 8, iota((16, columns), 1)
    for c in range(CLASSES):
        part = pl.ds(c * modes, modes)
        first = jnp.logical_and(line == 2 * c, lane == 0)
        last = jnp.logical_and(line == 2 * c + 1, lane == columns - 1)
        base_ref[part] = base_ref[part] + dot(added, jnp.logical_or(first, last).astype(BF16))


def ends(thermal, inner, high, low, ring, beyond):
    return pl.pallas_call(
        ends_kernel,
        in_specs=[SMEM] + [VMEM] * 5,
        out_shape=pltpu.VMEM(inner.shape, F32),
        out_specs=VMEM,
        input_output_aliases={1: 0},
        compiler_params=PARAMS,
        name="ends",
    )(thermal, inner, high, low, ring, beyond)


def place_kernel(target_ref, _, *refs):
    arrived, (collision_ref, base_ref, out_hbm, collision_hbm, sems) = refs[:-5], refs[-5:]
    terms = arrived[0].shape[0]
    me, group = lax.axis_index("mode"), lax.axis_size("mode")
    copies = [pltpu.make_async_copy(collision_ref, collision_hbm, sems.at[0])]
    for r, terms_ref in enumerate(arrived, 1):
        first = lax.rem(me + r, group) * terms
        values = collision_update * terms_ref[...].astype(F32)
        for j in range(terms):
            row = pl.ds(target_ref[first + j], 1)
            base_ref[row] = base_ref[row] + values[j : j + 1]
    copies.append(pltpu.make_async_copy(base_ref, out_hbm, sems.at[1]))
    copies[1].start()
    copies[0].start()
    for copy in copies:
        copy.wait()


def place(target, base, arrived, collision):
    return pl.pallas_call(
        place_kernel,
        in_specs=[SMEM, VMEM] + [VMEM] * (len(arrived) + 1),
        out_shape=(
            pltpu.VMEM(base.shape, F32),
            jax.ShapeDtypeStruct(base.shape, F32),
            jax.ShapeDtypeStruct(collision.shape, F32),
        ),
        out_specs=(VMEM, HBM, HBM),
        scratch_shapes=[pltpu.SemaphoreType.DMA((2,))],
        input_output_aliases={1: 0},
        compiler_params=PARAMS,
        name="place",
    )(target, base, *arrived, collision)


def shards(state, tensor, table, thermal, output_mode_row):
    rows = state.shape[0]
    terms, modes, _ = tensor.shape
    slabs, group = lax.axis_size("space"), lax.axis_size("mode")

    def shift(x, by):
        return lax.ppermute(x, "mode", [(i, (i + by) % group) for i in range(group)])

    columns = state.shape[1]
    flat = remain(jnp.transpose(tensor, (1, 0, 2)).reshape(modes * terms, rows))
    coarse, wide, index, speed, target, *held = coarsen(state, table.T, thermal, output_mode_row, flat)
    given = wide, index, speed, target, flat
    cells = [coarse] + [shift(coarse, r) for r in range(1, group)]

    lines = -(-rows // columns // 8) * 8
    edge, *held = preparing(early_kernel, *given, held, [coarse], extra=[pltpu.VMEM((lines, columns), BF16)])
    size = slabs * group
    pairs = [(s * group + group - 1, (s + 1) * group % size) for s in range(slabs)]
    ring = lax.ppermute(edge, ("space", "mode"), pairs + [(j, i) for i, j in pairs])
    held_tensor, high, low, inner, kind, own = preparing(late_kernel, *given, held)

    totals, sent = collide(held_tensor, kind, own, cells)
    arrived = [shift(x, group - r) for r, x in enumerate(sent, 1)]
    base, collision, beyond = own_ends(target, inner, cells[1], cells[group - 1], totals)
    base = ends(speed, base, high, low, ring, beyond)
    return place(target, base, arrived, collision)[1:]


def solution(mesh):
    in_specs = (P(None, ("space", "mode")), P("mode", None, None), P(), P(), P())
    out_specs = (P(None, ("space", "mode")), P("mode", "space"))
    return jax.shard_map(shards, mesh=mesh, in_specs=in_specs, out_specs=out_specs, check_vma=False)
```
